256 devices in a mesh: layer: 2 (over core), rows: 128 (over y, x, z).
Axes of the slice: x: 4, y: 4, z: 8, core: 2. Of those that a mesh axis runs over, the one named last changes fastest.
Arguments:
- frames: bfloat16 [3, 256, 256, 256], P(None, 'rows'), may hold values from -6 to 6
- initial_state: bfloat16 [2, 256, 256, 256], P('layer', 'rows'), may hold values from -3 to 3
- w_gates: bfloat16 [2, 3, 3, 512, 512], P('layer'), may hold values from -0.25 to 0.25
- w_cand: bfloat16 [2, 3, 3, 512, 256], P('layer'), may hold values from -0.125 to 0.125
- biases: float32 [2, 768], P('layer'), may hold values from -4 to 4
Outputs:
- hidden_frames: bfloat16 [2, 3, 256, 256, 256], P('layer', None, 'rows')
The draws below stay inside these ranges and needn't reach their ends.
All inputs are finite; a program needn't handle non-finite values.
Results may differ from the reference program's by a relative error of at most 0.0048.
Values may be sent and summed in bfloat16 or wider, within the bound.
No kernel may reach another device: no remote copies, remote signals or barrier semaphores. Data moves between devices by JAX's collectives and lax.ppermute only.
A program may use at most 64 MiB of HBM per device.

```python
import jax
import jax.numpy as jnp

CH = 256
COLS = 256
FRAMES = 3
LAYERS = 2
GRID_ROWS = 256


def block_scale(key, dims, cuts, low, largest):
    def one(position, shards_of):
        draws = jax.random.uniform(jax.random.fold_in(jax.random.fold_in(key, 6), position), (shards_of,), jnp.float32, low / len(cuts), largest / len(cuts))
        return jnp.repeat(jnp.exp(draws), dims[position] // shards_of).reshape((-1,) + (1,) * (len(dims) - position - 1))

    factor_of = one(*cuts[0])
    for cut in cuts[1:]:
        factor_of = factor_of * one(*cut)
    return factor_of


def normal_values(rng, extent, width, limit, cuts=(), held_as=jnp.bfloat16):
    values = width * jax.random.normal(rng, extent, jnp.float32)
    if cuts:
        values = values * block_scale(rng, extent, cuts, -0.22, 0.18)
    return jnp.clip(values, -limit, limit).astype(held_as)


def setup_inputs(seed: int = 0) -> dict:
    arg_keys = jax.random.split(jax.random.key(seed), 6)
    return {
        "frames": normal_values(arg_keys[0], (FRAMES, GRID_ROWS, COLS, CH), 1.0, 6.0, ((1, 128),)),
        "initial_state": normal_values(arg_keys[1], (LAYERS, GRID_ROWS, COLS, CH), 1.2, 3.0, ((0, 2), (1, 128))),
        "w_gates": normal_values(arg_keys[2], (LAYERS, 3, 3, 2 * CH, 2 * CH), (5 * CH // 2) ** -0.5, 0.25, ((0, 2),)),
        "w_cand": normal_values(arg_keys[3], (LAYERS, 3, 3, 2 * CH, CH), (9 * CH) ** -0.5, 0.125, ((0, 2),)),
        "biases": normal_values(arg_keys[4], (LAYERS, 3 * CH), 1.0, 4.0, ((0, 2),), jnp.float32),
    }


def convolve(source_rows, weight):
    row_count, col_count, _ = source_rows.shape
    padded = jnp.pad(source_rows, ((1, 1), (1, 1), (0, 0)))
    summed = jnp.zeros((row_count * col_count, weight.shape[3]), jnp.float32)
    for row_off in range(3):
        for col_off in range(3):
            tap_view = padded[row_off:row_off + row_count, col_off:col_off + col_count].reshape(row_count * col_count, -1)
            summed = summed + jnp.dot(tap_view, weight[row_off, col_off], preferred_element_type=jnp.float32)
    return summed.reshape(row_count, col_count, -1)


def reference(frames, initial_state, w_gates, w_cand, biases):
    channels = initial_state.shape[-1]
    sequence = frames
    collected = []
    for layer_idx in range(LAYERS):
        hidden = initial_state[layer_idx]
        produced = []
        for frame_idx in range(FRAMES):
            inputs = sequence[frame_idx]
            gate_pre = convolve(jnp.concatenate([inputs, hidden], -1), w_gates[layer_idx]) + biases[layer_idx, :2 * channels]
            gate_all = jax.nn.sigmoid(gate_pre)
            update = gate_all[..., :channels]
            reset_gate = gate_all[..., channels:]
            reset_state = (reset_gate * hidden.astype(jnp.float32)).astype(jnp.bfloat16)
            candidate = jnp.tanh(convolve(jnp.concatenate([inputs, reset_state], -1), w_cand[layer_idx]) + biases[layer_idx, 2 * channels:])
            hidden = ((1.0 - update) * hidden.astype(jnp.float32) + update * candidate).astype(jnp.bfloat16)
            produced.append(hidden)
        sequence = jnp.stack(produced)
        collected.append(sequence)
    return jnp.stack(collected)
```

```python
import functools

import jax
import jax.numpy as jnp
from jax import lax
from jax.experimental import pallas as pl
from jax.experimental.pallas import tpu as pltpu
from jax.sharding import PartitionSpec as P

VMEM_BYTES = 26 * 1024 * 1024


def widen(target, row, value):
    cols, channels = value.shape
    wide = value.astype(jnp.float32)
    position = lax.broadcasted_iota(jnp.int32, (cols, channels), 0)
    left = jnp.where(position == 0, 0.0, pltpu.roll(wide, 1, 0))
    right = jnp.where(position == cols - 1, 0.0, pltpu.roll(wide, cols - 1, 0))
    target[row, :, 0:channels] = left.astype(jnp.bfloat16)
    target[row, :, channels : 2 * channels] = value
    target[row, :, 2 * channels : 3 * channels] = right.astype(jnp.bfloat16)


def fill(target, own, first, second, odd):
    for row in range(2):
        widen(target, row, jnp.where(odd, first[row], second[row]))
        widen(target, row + 2, own[row])
        widen(target, row + 4, jnp.where(odd, second[row], first[row]))


def taps(source, start, rows, weight, lo, out_lo, channels):
    cols = source.shape[1]
    total = None
    for row_off in range(3):
        view = source[start + row_off : start + row_off + rows].reshape(rows * cols, 3 * channels)
        kernel = weight[row_off, :, lo : lo + channels, out_lo : out_lo + channels]
        part = jnp.dot(
            view, kernel.reshape(3 * channels, channels), preferred_element_type=jnp.float32
        )
        total = part if total is None else total + part
    return total


def step_kernel(
    lag, flags, own, first, second, x0, x0a, x0b, x1, x1h, wg, wc, bias, out,
    wide_h, wide_x, wide_r, pre_r, pre_u, pre_c,
):
    layer, odd = flags[0], flags[1] == 1
    cols, channels = own.shape[1:]
    if lag == 0:
        active = layer == 0
    elif lag == 3:
        active = layer == 1
    else:
        active = layer >= 0

    @pl.when(jnp.logical_not(active))
    def _():
        out[...] = own[...]

    @pl.when(active)
    def _():
        fill(wide_h, own, first, second, odd)
        pre_r[...] = taps(wide_h, 0, 4, wg, channels, channels, channels)
        pre_u[...] = taps(wide_h, 1, 2, wg, channels, 0, channels)

        if lag < 3:
            @pl.when(layer == 0)
            def _():
                fill(wide_x, x0, x0a, x0b, odd)

        if lag > 0:
            @pl.when(layer == 1)
            def _():
                fill(wide_x, x1, x1h.at[0:2], x1h.at[2:4], odd)

        pre_r[...] += taps(wide_x, 0, 4, wg, 0, channels, channels)
        pre_u[...] += taps(wide_x, 1, 2, wg, 0, 0, channels)
        pre_c[...] = taps(wide_x, 1, 2, wc, 0, 0, channels)
        for row in range(4):
            held = wide_h[row + 1, :, channels : 2 * channels].astype(jnp.float32)
            gate = jax.nn.sigmoid(
                pre_r[row * cols : (row + 1) * cols] + bias[:, channels : 2 * channels]
            )
            widen(wide_r, row, (gate * held).astype(jnp.bfloat16))
        pre_c[...] += taps(wide_r, 0, 2, wc, channels, 0, channels)
        for row in range(2):
            part = slice(row * cols, (row + 1) * cols)
            held = own[row].astype(jnp.float32)
            update = jax.nn.sigmoid(pre_u[part] + bias[:, 0:channels])
            candidate = jnp.tanh(pre_c[part] + bias[:, 2 * channels : 3 * channels])
            out[row] = ((1.0 - update) * held + update * candidate).astype(jnp.bfloat16)


def gru_step(lag, flags, own, first, second, x0, x0a, x0b, x1, x1h, wg, wc, bias):
    rows, cols, channels = own.shape
    wide = lambda n: pltpu.VMEM((n, cols, 3 * channels), jnp.bfloat16)
    pre = lambda n: pltpu.VMEM((n * cols, channels), jnp.float32)
    held = pl.BlockSpec(memory_space=pltpu.VMEM)
    return pl.pallas_call(
        functools.partial(step_kernel, lag),
        out_shape=jax.ShapeDtypeStruct(own.shape, own.dtype),
        in_specs=[pl.BlockSpec(memory_space=pltpu.SMEM)] + [held] * 11,
        out_specs=held,
        scratch_shapes=[wide(6), wide(6), wide(4), pre(4), pre(2), pre(2)],
        compiler_params=pltpu.CompilerParams(vmem_limit_bytes=VMEM_BYTES),
        cost_estimate=pl.CostEstimate(
            flops=2 * 8 * cols * channels * 9 * channels, bytes_accessed=8 << 20, transcendentals=0
        ),
    )(flags, own, first, second, x0, x0a, x0b, x1, x1h, wg, wc, bias)


def pairs(count, start, offset):
    found = []
    for low in range(start, count - 1, 2):
        found += [(offset + low, offset + low + 1), (offset + low + 1, offset + low)]
    return found


def swap(field, layers):
    count = lax.axis_size("rows")
    route = lambda start: [p for layer in layers for p in pairs(count, start, layer * count)]
    names = ("layer", "rows")
    return lax.ppermute(field, names, route(0)), lax.ppermute(field, names, route(1))


def shards(frames, initial_state, w_gates, w_cand, biases):
    layer = lax.axis_index("layer")
    strip = lax.axis_index("rows")
    flags = jnp.stack([layer, lax.rem(strip, 2)]).astype(jnp.int32)
    wg, wc = w_gates[0], w_cand[0]
    hidden = initial_state[0]
    up = [(0, 1)]
    down = [(1, 0)]

    first, second = swap(jnp.where(layer == 0, hidden, frames[0]), (0, 1))
    halo = lax.ppermute(jnp.concatenate([first, second]), "layer", down)
    later_a, later_b = swap(frames[1:3].reshape((4,) + hidden.shape[1:]), (1,))
    later = lax.ppermute(jnp.concatenate([later_a, later_b]), "layer", down)
    frame_halos = [
        (halo[0:2], halo[2:4]),
        (later[0:2], later[4:6]),
        (later[2:4], later[6:8]),
    ]
    x1 = hidden
    x1h = halo
    states = []
    for step in range(4):
        frame = min(step, 2)
        x0a, x0b = frame_halos[frame]
        hidden = gru_step(
            step, flags, hidden, first, second, frames[frame], x0a, x0b, x1, x1h, wg, wc, biases
        )
        states.append(hidden)
        if step < 3:
            x1 = lax.ppermute(hidden, "layer", up)
            first, second = swap(hidden, (0, 1))
            x1h = lax.ppermute(jnp.concatenate([first, second]), "layer", up)
    out = [
        jnp.where(layer == 0, states[0], states[1]),
        jnp.where(layer == 0, states[1], states[2]),
        states[3],
    ]
    return jnp.stack(out)[None]


def solution(mesh):
    placed = (
        P(None, "rows", None, None),
        P("layer", "rows", None, None),
        P("layer", None, None, None, None),
        P("layer", None, None, None, None),
        P("layer", None),
    )
    return jax.shard_map(
        shards,
        mesh=mesh,
        in_specs=placed,
        out_specs=P("layer", None, "rows", None, None),
        check_vma=False,
    )
```

```python
import functools

import jax
import jax.numpy as jnp
from jax import lax
from jax.experimental import pallas as pl
from jax.experimental.pallas import tpu as pltpu
from jax.sharding import PartitionSpec as P

MIB = 1024 * 1024


def widen(target, row, value):
    cols, channels = value.shape
    wide = value.astype(jnp.float32)
    position = lax.broadcasted_iota(jnp.int32, (cols, channels), 0)
    left = jnp.where(position == 0, 0.0, pltpu.roll(wide, 1, 0))
    right = jnp.where(position == cols - 1, 0.0, pltpu.roll(wide, cols - 1, 0))
    target[row, :, 0:channels] = left.astype(jnp.bfloat16)
    target[row, :, channels : 2 * channels] = value
    target[row, :, 2 * channels : 3 * channels] = right.astype(jnp.bfloat16)


def halo_row(first, second, odd, row, base=0):
    one, other = first[base + row % 2], second[base + row % 2]
    return jnp.where(odd == (row < 2), one, other)


def fill(target, own, first, second, odd, own_base, halo_base):
    for row in range(2):
        widen(target, row, halo_row(first, second, odd, row, halo_base))
        widen(target, row + 2, own[own_base + row])
        widen(target, row + 4, halo_row(first, second, odd, row + 2, halo_base))


def taps(source, start, rows, weight, lo, out_lo, channels):
    cols = source.shape[1]
    total = None
    for row_off in range(3):
        view = source[start + row_off : start + row_off + rows].reshape(rows * cols, 3 * channels)
        kernel = weight[row_off, :, lo : lo + channels, out_lo : out_lo + channels]
        part = jnp.dot(
            view, kernel.reshape(3 * channels, channels), preferred_element_type=jnp.float32
        )
        total = part if total is None else total + part
    return total


def early_kernel(
    role, bases, of_state, flags, own, first, second, wg, wc, *rest
):
    pre_r, pre_u = rest[:2]
    channels = own.shape[-1]
    lo = channels if of_state else 0

    @pl.when(flags[0] == role)
    def _():
        wide = rest[-1]
        fill(wide, own, first, second, flags[1] == 1, *bases)
        pre_r[...] = taps(wide, 0, 4, wg, lo, channels, channels)
        pre_u[...] = taps(wide, 1, 2, wg, lo, 0, channels)
        if not of_state:
            rest[2][...] = taps(wide, 1, 2, wc, 0, 0, channels)


def late_kernel(role, bases, of_state, with_other, flags, state, source, pre, weights, rest):
    own, first, second = state
    wg, wc, bias = weights
    out, wide, wide_r, sum_c = rest[-4:]
    cols, channels = own.shape[1:]
    lo = channels if of_state else 0

    @pl.when(flags[0] == role)
    def _():
        odd = flags[1] == 1
        fill(wide, *source, odd, *bases)
        sum_r = pre[0][...] + taps(wide, 0, 4, wg, lo, channels, channels)
        for row in range(4):
            held = own[row - 1] if 0 < row < 3 else halo_row(first, second, odd, 1 if row == 0 else 2)
            gate = jax.nn.sigmoid(
                sum_r[row * cols : (row + 1) * cols] + bias[:, channels : 2 * channels]
            )
            widen(wide_r, row, (gate * held.astype(jnp.float32)).astype(jnp.bfloat16))
        sum_u = pre[1][...] + taps(wide, 1, 2, wg, lo, 0, channels)
        of_input = pre[2][...] if of_state else taps(wide, 1, 2, wc, 0, 0, channels)
        sum_c[...] = of_input + taps(wide_r, 0, 2, wc, channels, 0, channels)
        for row in range(2):
            part = slice(row * cols, (row + 1) * cols)
            held = own[row].astype(jnp.float32)
            update = jax.nn.sigmoid(sum_u[part] + bias[:, 0:channels])
            candidate = jnp.tanh(sum_c[part] + bias[:, 2 * channels : 3 * channels])
            out[row] = ((1.0 - update) * held + update * candidate).astype(jnp.bfloat16)

    if with_other:
        @pl.when(flags[0] != role)
        def _():
            out[...] = rest[0][...]


HELD = pl.BlockSpec(memory_space=pltpu.VMEM)
SCALARS = pl.BlockSpec(memory_space=pltpu.SMEM)


def cost(cols, channels):
    return pl.CostEstimate(
        flops=2 * 8 * cols * channels * 9 * channels, bytes_accessed=1 << 20, transcendentals=0
    )


def early(role, flags, source, wg, wc, bases=(0, 0), of_state=False):
    cols, channels = source[0].shape[1:]
    pre = lambda n: jax.ShapeDtypeStruct((n * cols, channels), jnp.float32)
    shapes = [pre(4), pre(2)] + ([] if of_state else [pre(2)])
    return pl.pallas_call(
        functools.partial(early_kernel, role, bases, of_state),
        out_shape=shapes,
        in_specs=[SCALARS] + [HELD] * 5,
        out_specs=[HELD] * len(shapes),
        scratch_shapes=[pltpu.VMEM((6, cols, 3 * channels), jnp.bfloat16)],
        compiler_params=pltpu.CompilerParams(vmem_limit_bytes=8 * MIB),
        cost_estimate=cost(cols, channels),
    )(flags, *source, wg, wc)


def late(role, flags, state, pre, wg, wc, bias, other=None, source=None, bases=(0, 0)):
    _, cols, channels = state[0].shape
    of_state = source is None
    operands = [*state, *([] if of_state else source), *pre, wg, wc, bias]
    if other is not None:
        operands.append(other)

    def kernel(scalars, *refs):
        held = refs[0:3]
        used = 3 if of_state else 6
        sums = refs[used : used + len(pre)]
        used += len(pre)
        late_kernel(
            role, bases, of_state, other is not None, scalars, held,
            held if of_state else refs[3:6], sums, refs[used : used + 3], refs[used + 3 :],
        )

    return pl.pallas_call(
        kernel,
        out_shape=jax.ShapeDtypeStruct((2, cols, channels), jnp.bfloat16),
        in_specs=[SCALARS] + [HELD] * len(operands),
        out_specs=HELD,
        scratch_shapes=[
            pltpu.VMEM((6, cols, 3 * channels), jnp.bfloat16),
            pltpu.VMEM((4, cols, 3 * channels), jnp.bfloat16),
            pltpu.VMEM((2 * cols, channels), jnp.float32),
        ],
        compiler_params=pltpu.CompilerParams(vmem_limit_bytes=12 * MIB),
        cost_estimate=cost(cols, channels),
    )(flags, *operands)


def swap(field, source, target):
    count = lax.axis_size("rows")

    def route(start):
        found = []
        for low in range(start, count - 1, 2):
            for here, there in ((low, low + 1), (low + 1, low)):
                found.append((source * count + here, target * count + there))
        return found

    names = ("layer", "rows")
    return lax.ppermute(field, names, route(0)), lax.ppermute(field, names, route(1))


def across(field, source):
    return lax.ppermute(field, "layer", [(source, 1 - source)])


def after(value, *others):
    return lax.optimization_barrier((value, *others))[0]


def shards(frames, initial_state, w_gates, w_cand, biases):
    layer = lax.axis_index("layer")
    strip = lax.axis_index("rows")
    flags = jnp.stack([layer, lax.rem(strip, 2)]).astype(jnp.int32)
    wg, wc = w_gates[0], w_cand[0]
    initial = initial_state[0]

    rows = frames.reshape((6,) + initial.shape[1:])
    halo0 = swap(initial, 0, 0)
    frame_halos = swap(rows[0:4], 1, 0)
    halo1 = swap(initial, 1, 1)
    last_halos = swap(rows[4:6], 1, 0)

    low, high = [], []
    state = (after(initial, *halo1), *halo0)
    pre = early(0, flags, state, wg, wc, of_state=True)
    low.append(late(0, flags, state, pre, wg, wc, biases, source=(rows, *frame_halos)))
    crossing = None
    hidden1 = initial
    for frame in range(3):
        below = across(low[frame], 0)
        below_halo = swap(low[frame], 0, 1)
        if frame < 2:
            halos, base = ((frame_halos, 2), (last_halos, 0))[frame]
            pre = early(
                0, flags, (after(rows, low[frame]), *halos), wg, wc, (2 * frame + 2, base)
            )
            halo0 = [across(h, 1) for h in below_halo]
            own = low[frame] if crossing is None else after(low[frame], *crossing)
            low.append(late(0, flags, (own, *halo0), pre, wg, wc, biases))
        if crossing is not None:
            halo1 = [across(h, 0) for h in crossing]
        if frame < 2:
            below = after(below, low[frame + 1])
        pre1 = early(1, flags, (below, *below_halo), wg, wc)
        hidden1 = late(
            1, flags, (hidden1, *halo1), pre1, wg, wc, biases, low[frame] if frame == 2 else None
        )
        high.append(hidden1)
        if frame < 2:
            crossing = swap(hidden1, 1, 0)
    out = jnp.zeros((3,) + initial.shape, initial.dtype)
    for frame in range(3):
        result = high[2] if frame == 2 else jnp.where(layer == 0, low[frame], high[frame])
        out = lax.dynamic_update_slice(out, result[None], (frame, 0, 0, 0))
    return out[None]


def solution(mesh):
    placed = (
        P(None, "rows", None, None),
        P("layer", "rows", None, None),
        P("layer", None, None, None, None),
        P("layer", None, None, None, None),
        P("layer", None),
    )
    return jax.shard_map(
        shards,
        mesh=mesh,
        in_specs=placed,
        out_specs=P("layer", None, "rows", None, None),
        check_vma=False,
    )
```

```python
import functools

import jax
import jax.numpy as jnp
from jax import lax
from jax.experimental import pallas as pl
from jax.experimental.pallas import tpu as pltpu
from jax.sharding import PartitionSpec as P

VMEM_BYTES = 16 * 1024 * 1024


def widen(target, row, value):
    cols, channels = value.shape
    wide = value.astype(jnp.float32)
    position = lax.broadcasted_iota(jnp.int32, (cols, channels), 0)
    left = jnp.where(position == 0, 0.0, pltpu.roll(wide, 1, 0))
    right = jnp.where(position == cols - 1, 0.0, pltpu.roll(wide, cols - 1, 0))
    target[row, :, 0:channels] = left.astype(jnp.bfloat16)
    target[row, :, channels : 2 * channels] = value
    target[row, :, 2 * channels : 3 * channels] = right.astype(jnp.bfloat16)


def halo_row(first, second, odd, row):
    one, other = first[row % 2], second[row % 2]
    return jnp.where(odd == (row < 2), one, other)


def fill(target, own, first, second, odd, base=0):
    for row in range(2):
        widen(target, row, halo_row(first, second, odd, row))
        widen(target, row + 2, own[base + row])
        widen(target, row + 4, halo_row(first, second, odd, row + 2))


def taps(source, start, rows, weight, lo, out_lo, channels):
    cols = source.shape[1]
    total = None
    for row_off in range(3):
        view = source[start + row_off : start + row_off + rows].reshape(rows * cols, 3 * channels)
        kernel = weight[row_off, :, lo : lo + channels, out_lo : out_lo + channels]
        part = jnp.dot(
            view, kernel.reshape(3 * channels, channels), preferred_element_type=jnp.float32
        )
        total = part if total is None else total + part
    return total


def active(lag, layer):
    return layer == 0 if lag == 0 else layer == 1 if lag == 3 else layer >= 0


def early_kernel(lag, flags, own, first, second, wg, pre_r, pre_u, wide):
    channels = own.shape[-1]

    @pl.when(active(lag, flags[0]))
    def _():
        fill(wide, own, first, second, flags[1] == 1)
        pre_r[...] = taps(wide, 0, 4, wg, channels, channels, channels)
        pre_u[...] = taps(wide, 1, 2, wg, channels, 0, channels)


def late_kernel(
    lag, flags, own, first, second, pre_r, pre_u, x0, x0a, x0b, x1, x1a, x1b, wg, wc, bias, out,
    wide, wide_r, sum_c,
):
    cols, channels = own.shape[1:]
    layer, odd = flags[0], flags[1] == 1

    @pl.when(active(lag, layer))
    def _():
        if lag < 3:
            @pl.when(layer == 0)
            def _():
                fill(wide, x0, x0a, x0b, odd, 2 * lag)

        if lag > 0:
            @pl.when(layer == 1)
            def _():
                fill(wide, x1, x1a, x1b, odd)

        sum_r = pre_r[...] + taps(wide, 0, 4, wg, 0, channels, channels)
        for row in range(4):
            held = own[row - 1] if 0 < row < 3 else halo_row(first, second, odd, 1 if row == 0 else 2)
            gate = jax.nn.sigmoid(
                sum_r[row * cols : (row + 1) * cols] + bias[:, channels : 2 * channels]
            )
            widen(wide_r, row, (gate * held.astype(jnp.float32)).astype(jnp.bfloat16))
        sum_u = pre_u[...] + taps(wide, 1, 2, wg, 0, 0, channels)
        of_input = taps(wide, 1, 2, wc, 0, 0, channels)
        sum_c[...] = of_input + taps(wide_r, 0, 2, wc, channels, 0, channels)
        for row in range(2):
            part = slice(row * cols, (row + 1) * cols)
            held = own[row].astype(jnp.float32)
            update = jax.nn.sigmoid(sum_u[part] + bias[:, 0:channels])
            candidate = jnp.tanh(sum_c[part] + bias[:, 2 * channels : 3 * channels])
            out[row] = ((1.0 - update) * held + update * candidate).astype(jnp.bfloat16)

    if lag in (0, 3):
        @pl.when(jnp.logical_not(active(lag, layer)))
        def _():
            out[...] = own[...]


HELD = pl.BlockSpec(memory_space=pltpu.VMEM)
SCALARS = pl.BlockSpec(memory_space=pltpu.SMEM)


def cost(cols, channels):
    return pl.CostEstimate(
        flops=2 * 8 * cols * channels * 9 * channels, bytes_accessed=1 << 20, transcendentals=0
    )


def early(lag, flags, state, wg):
    _, cols, channels = state[0].shape
    pre = lambda n: jax.ShapeDtypeStruct((n * cols, channels), jnp.float32)
    return pl.pallas_call(
        functools.partial(early_kernel, lag),
        out_shape=[pre(4), pre(2)],
        in_specs=[SCALARS] + [HELD] * 4,
        out_specs=[HELD] * 2,
        scratch_shapes=[pltpu.VMEM((6, cols, 3 * channels), jnp.bfloat16)],
        compiler_params=pltpu.CompilerParams(vmem_limit_bytes=VMEM_BYTES),
        cost_estimate=cost(cols, channels),
    )(flags, *state, wg)


def late(lag, flags, state, pre, x0, x1, wg, wc, bias):
    _, cols, channels = state[0].shape
    return pl.pallas_call(
        functools.partial(late_kernel, lag),
        out_shape=jax.ShapeDtypeStruct((2, cols, channels), jnp.bfloat16),
        in_specs=[SCALARS] + [HELD] * 14,
        out_specs=HELD,
        scratch_shapes=[
            pltpu.VMEM((6, cols, 3 * channels), jnp.bfloat16),
            pltpu.VMEM((4, cols, 3 * channels), jnp.bfloat16),
            pltpu.VMEM((2 * cols, channels), jnp.float32),
        ],
        compiler_params=pltpu.CompilerParams(vmem_limit_bytes=VMEM_BYTES),
        cost_estimate=cost(cols, channels),
    )(flags, *state, *pre, *x0, *x1, wg, wc, bias)


def pair_swap(field, start):
    count = lax.axis_size("rows")
    route = []
    for low in range(start, count - 1, 2):
        route += [(low, low + 1), (low + 1, low)]
    return lax.ppermute(field, "rows", route)


def gathered_swap(field, strip):
    count = lax.axis_size("rows")
    groups = [[0, count], [count - 1, 2 * count - 1]]
    for layer in range(2):
        groups += [[layer * count + low, layer * count + low + 1] for low in range(1, count - 1, 2)]
    both = lax.all_gather(field, ("layer", "rows"), axis_index_groups=groups)
    inner = jnp.logical_and(strip > 0, strip < count - 1)
    partner = jnp.where(lax.rem(strip, 2) == 1, both[1], both[0])
    return jnp.where(inner, partner, jnp.zeros_like(partner))


def across(field):
    return lax.ppermute(field, "layer", [(0, 1), (1, 0)])


def shards(frames, initial_state, w_gates, w_cand, biases):
    layer = lax.axis_index("layer")
    strip = lax.axis_index("rows")
    flags = jnp.stack([layer, lax.rem(strip, 2)]).astype(jnp.int32)
    wg, wc = w_gates[0], w_cand[0]
    hidden = initial_state[0]
    rows = frames.reshape((6,) + hidden.shape[1:])

    field = jnp.where(layer == 0, hidden, frames[0])
    first, second = pair_swap(field, 0), pair_swap(field, 1)
    field = jnp.where(layer == 0, frames[1], frames[2])
    late_first, late_second = pair_swap(field, 0), pair_swap(field, 1)
    halos = [
        (across(first), across(second)),
        (late_first, late_second),
        (across(late_first), across(late_second)),
    ]
    below = (hidden, first, second)
    states = []
    for step in range(4):
        state = (hidden, first, second)
        pre = early(step, flags, state, wg)
        own_halos = halos[min(step, 2)]
        hidden = late(step, flags, state, pre, (rows, *own_halos), below, wg, wc, biases)
        states.append(hidden)
        if step < 3:
            first = pair_swap(hidden, 0)
            own_below = across(hidden)
            second = gathered_swap(hidden, strip)
            below = (own_below, across(first), across(second))
    out = jnp.stack(
        [
            jnp.where(layer == 0, states[0], states[1]),
            jnp.where(layer == 0, states[1], states[2]),
            jnp.zeros_like(hidden),
        ]
    )
    return lax.dynamic_update_slice(out, states[3][None], (2, 0, 0, 0))[None]


def solution(mesh):
    placed = (
        P(None, "rows", None, None),
        P("layer", "rows", None, None),
        P("layer", None, None, None, None),
        P("layer", None, None, None, None),
        P("layer", None),
    )
    return jax.shard_map(
        shards,
        mesh=mesh,
        in_specs=placed,
        out_specs=P("layer", None, "rows", None, None),
        check_vma=False,
    )
```

```python
import functools

import jax
import jax.numpy as jnp
from jax import lax
from jax.experimental import pallas as pl
from jax.experimental.pallas import tpu as pltpu
from jax.sharding import PartitionSpec as P

VMEM_BYTES = 16 * 1024 * 1024


def widen(target, row, value):
    cols, channels = value.shape
    wide = value.astype(jnp.float32)
    position = lax.broadcasted_iota(jnp.int32, (cols, channels), 0)
    left = jnp.where(position == 0, 0.0, pltpu.roll(wide, 1, 0))
    right = jnp.where(position == cols - 1, 0.0, pltpu.roll(wide, cols - 1, 0))
    target[row, :, 0:channels] = left.astype(jnp.bfloat16)
    target[row, :, channels : 2 * channels] = value
    target[row, :, 2 * channels : 3 * channels] = right.astype(jnp.bfloat16)


def halo_row(first, second, odd, row):
    one, other = first[row % 2], second[row % 2]
    return jnp.where(odd == (row < 2), one, other)


def fill(target, own, first, second, odd, base=0):
    for row in range(2):
        widen(target, row, halo_row(first, second, odd, row))
        widen(target, row + 2, own[base + row])
        widen(target, row + 4, halo_row(first, second, odd, row + 2))


def taps(source, start, rows):
    _, cols, width = source.shape
    return jnp.concatenate(
        [source[start + tap : start + tap + rows].reshape(rows * cols, width) for tap in range(3)],
        -1,
    )


def columns(weight, lo, channels, out_lo, out_hi):
    return weight[:, :, lo : lo + channels, out_lo:out_hi].reshape(9 * channels, out_hi - out_lo)


def product(left, right):
    return jnp.dot(left, right, preferred_element_type=jnp.float32)


def active(lag, layer):
    return layer == 0 if lag == 0 else layer == 1 if lag == 3 else layer >= 0


def is_odd():
    return lax.rem(lax.axis_index("rows"), 2) == 1


def early_kernel(lag, own, first, second, wg, pre_r, pre_u, wide, *streamed):
    cols, channels = own.shape[1:]

    @pl.when(active(lag, lax.axis_index("layer")))
    def _():
        lo = channels
        weight = wg
        if streamed:
            weight, ready = streamed
            copy = pltpu.make_async_copy(wg.at[:, :, channels : 2 * channels], weight, ready)
            copy.start()
            lo = 0
        fill(wide, own, first, second, is_odd())
        if streamed:
            copy.wait()
        inner = product(taps(wide, 1, 2), columns(weight, lo, channels, 0, 2 * channels))
        edges = jnp.concatenate([taps(wide, 0, 1), taps(wide, 3, 1)], 0)
        outer = product(edges, columns(weight, lo, channels, channels, 2 * channels))
        pre_u[...] = inner[:, 0:channels]
        pre_r[cols : 3 * cols] = inner[:, channels : 2 * channels]
        pre_r[0:cols] = outer[0:cols]
        pre_r[3 * cols : 4 * cols] = outer[cols : 2 * cols]


def late_body(lag, own, first, second, pre, x0, x1, wg, wc, bias, wide, wide_r, store):
    cols, channels = own.shape[1:]
    layer, odd = lax.axis_index("layer"), is_odd()
    if lag < 3:
        @pl.when(layer == 0)
        def _():
            fill(wide, *x0, odd, 2 * lag)

    if lag > 0:
        @pl.when(layer == 1)
        def _():
            fill(wide, *x1, odd)

    of_reset = product(taps(wide, 0, 4), columns(wg, 0, channels, channels, 2 * channels))
    for row in range(4):
        part = slice(row * cols, (row + 1) * cols)
        held = own[row - 1] if 0 < row < 3 else halo_row(first, second, odd, 1 if row == 0 else 2)
        gate = jax.nn.sigmoid(
            pre[0][part] + of_reset[part] + bias[:, channels : 2 * channels]
        )
        widen(wide_r, row, (gate * held.astype(jnp.float32)).astype(jnp.bfloat16))
    weight = jnp.concatenate(
        [columns(wg, 0, channels, 0, channels), columns(wc, 0, channels, 0, channels)], -1
    )
    inner = product(taps(wide, 1, 2), weight)
    sum_u = pre[1][...] + inner[:, 0:channels]
    sum_c = inner[:, channels : 2 * channels] + product(
        taps(wide_r, 0, 2), columns(wc, channels, channels, 0, channels)
    )
    for row in range(2):
        part = slice(row * cols, (row + 1) * cols)
        held = own[row].astype(jnp.float32)
        update = jax.nn.sigmoid(sum_u[part] + bias[:, 0:channels])
        candidate = jnp.tanh(sum_c[part] + bias[:, 2 * channels : 3 * channels])
        store(row, ((1.0 - update) * held + update * candidate).astype(jnp.bfloat16))


def late_kernel(lag, *refs):
    own, first, second, pre_r, pre_u = refs[0:5]
    x0, x1 = refs[5:8], refs[8:11]
    wg, wc, bias, out, wide, wide_r = refs[11:17]

    def store(row, value):
        out[row] = value

    @pl.when(active(lag, lax.axis_index("layer")))
    def _():
        late_body(
            lag, own, first, second, (pre_r, pre_u), x0, x1, wg, wc, bias, wide, wide_r, store
        )

    if lag == 0:
        @pl.when(lax.axis_index("layer") == 1)
        def _():
            out[...] = own[...]


def last_kernel(*refs):
    own, first, second, pre_r, pre_u = refs[0:5]
    x1 = refs[5:8]
    wg, wc, bias, state0, state1, out, wide, wide_r, result, sent = refs[8:18]
    layer = lax.axis_index("layer")

    @pl.when(layer == 0)
    def _():
        copies = [
            pltpu.make_async_copy(state, out.at[frame], sent.at[frame])
            for frame, state in enumerate((state0, state1, own))
        ]
        for copy in copies:
            copy.start()
        for copy in copies:
            copy.wait()

    @pl.when(layer == 1)
    def _():
        copies = [
            pltpu.make_async_copy(state, out.at[frame], sent.at[frame])
            for frame, state in enumerate((state1, own))
        ]
        for copy in copies:
            copy.start()

        def store(row, value):
            result[row] = value
            copy = pltpu.make_async_copy(result.at[row], out.at[2, row], sent.at[2 + row])
            copy.start()
            copies.append(copy)

        late_body(
            3, own, first, second, (pre_r, pre_u), None, x1, wg, wc, bias, wide, wide_r, store
        )
        for copy in copies:
            copy.wait()


HELD = pl.BlockSpec(memory_space=pltpu.VMEM)
ANYWHERE = pl.BlockSpec(memory_space=pl.ANY)
OUTSIDE = pl.BlockSpec(memory_space=pltpu.HBM)


def cost(units, cols, channels):
    return pl.CostEstimate(
        flops=2 * units * cols * channels * 9 * channels, bytes_accessed=1 << 20, transcendentals=0
    )


def wide_rows(rows, cols, channels):
    return pltpu.VMEM((rows, cols, 3 * channels), jnp.bfloat16)


def early(lag, state, wg):
    _, cols, channels = state[0].shape
    pre = lambda n: jax.ShapeDtypeStruct((n * cols, channels), jnp.float32)
    scratch = [wide_rows(6, cols, channels)]
    if lag == 0:
        scratch += [
            pltpu.VMEM((3, 3, channels, 2 * channels), jnp.bfloat16), pltpu.SemaphoreType.DMA
        ]
    if lag == 0:
        wg = pltpu.with_memory_space_constraint(wg, pltpu.HBM)
    return pl.pallas_call(
        functools.partial(early_kernel, lag),
        out_shape=[pre(4), pre(2)],
        in_specs=[HELD] * 3 + [OUTSIDE if lag == 0 else HELD],
        out_specs=[HELD] * 2,
        scratch_shapes=scratch,
        compiler_params=pltpu.CompilerParams(vmem_limit_bytes=VMEM_BYTES),
        cost_estimate=cost(6, cols, channels),
    )(*state, wg)


def late(lag, state, pre, x0, x1, wg, wc, bias):
    _, cols, channels = state[0].shape
    return pl.pallas_call(
        functools.partial(late_kernel, lag),
        out_shape=jax.ShapeDtypeStruct((2, cols, channels), jnp.bfloat16),
        in_specs=[HELD] * 14,
        out_specs=HELD,
        scratch_shapes=[wide_rows(6, cols, channels), wide_rows(4, cols, channels)],
        compiler_params=pltpu.CompilerParams(vmem_limit_bytes=VMEM_BYTES),
        cost_estimate=cost(10, cols, channels),
    )(*state, *pre, *x0, *x1, wg, wc, bias)


def last(state, pre, x1, wg, wc, bias, earlier):
    _, cols, channels = state[0].shape
    return pl.pallas_call(
        last_kernel,
        out_shape=jax.ShapeDtypeStruct((3, 2, cols, channels), jnp.bfloat16),
        in_specs=[HELD] * 13,
        out_specs=ANYWHERE,
        scratch_shapes=[
            wide_rows(6, cols, channels),
            wide_rows(4, cols, channels),
            pltpu.VMEM((2, cols, channels), jnp.bfloat16),
            pltpu.SemaphoreType.DMA((4,)),
        ],
        compiler_params=pltpu.CompilerParams(vmem_limit_bytes=VMEM_BYTES),
        cost_estimate=cost(10, cols, channels),
    )(*state, *pre, *x1, wg, wc, bias, *earlier)


def pair_swap(field, start):
    count = lax.axis_size("rows")
    route = []
    for low in range(start, count - 1, 2):
        route += [(low, low + 1), (low + 1, low)]
    return lax.ppermute(field, "rows", route)


def gathered_swap(field, strip):
    count = lax.axis_size("rows")
    groups = [[0, count], [count - 1, 2 * count - 1]]
    for layer in range(2):
        groups += [[layer * count + low, layer * count + low + 1] for low in range(1, count - 1, 2)]
    both = lax.all_gather(field, ("layer", "rows"), axis_index_groups=groups)
    inner = jnp.logical_and(strip > 0, strip < count - 1)
    partner = jnp.where(lax.rem(strip, 2) == 1, both[1], both[0])
    return jnp.where(inner, partner, jnp.zeros_like(partner))


def across(field):
    return lax.ppermute(field, "layer", [(0, 1), (1, 0)])


def shards(frames, initial_state, w_gates, w_cand, biases):
    layer = lax.axis_index("layer")
    strip = lax.axis_index("rows")
    wg, wc = w_gates[0], w_cand[0]
    hidden = initial_state[0]
    rows = frames.reshape((6,) + hidden.shape[1:])

    field = jnp.where(layer == 0, hidden, frames[0])
    first, second = pair_swap(field, 0), pair_swap(field, 1)
    later_field = jnp.where(layer == 0, frames[1], frames[2])
    late_first, late_second = pair_swap(later_field, 0), pair_swap(later_field, 1)
    halos = [
        (across(first), across(second)),
        (late_first, late_second),
        (across(late_first), across(late_second)),
    ]
    below = (field, first, second)
    pre = early(0, below, wg)
    pre = lax.optimization_barrier((*pre, late_first, late_second))[0:2]
    hidden = late(0, (hidden, first, second), pre, (rows, *halos[0]), below, wg, wc, biases)
    states = [hidden]
    for step in range(1, 4):
        first = pair_swap(hidden, 0)
        own_below = across(hidden)
        second = gathered_swap(hidden, strip)
        below = (own_below, across(first), across(second))
        state = (hidden, first, second)
        pre = early(step, state, wg)
        if step == 3:
            return last(state, pre, below, wg, wc, biases, states[0:2])[None]
        hidden = late(step, state, pre, (rows, *halos[step]), below, wg, wc, biases)
        states.append(hidden)


def solution(mesh):
    placed = (
        P(None, "rows", None, None),
        P("layer", "rows", None, None),
        P("layer", None, None, None, None),
        P("layer", None, None, None, None),
        P("layer", None),
    )
    return jax.shard_map(
        shards,
        mesh=mesh,
        in_specs=placed,
        out_specs=P("layer", None, "rows", None, None),
        check_vma=False,
    )
```

```python
import functools

import jax
import jax.numpy as jnp
from jax import lax
from jax.experimental import pallas as pl
from jax.experimental.pallas import tpu as pltpu
from jax.sharding import PartitionSpec as P

VMEM_BYTES = 16 * 1024 * 1024
SMALL_BYTES = 8 * 1024 * 1024


def widen(target, row, value):
    cols, channels = value.shape
    wide = value.astype(jnp.float32)
    position = lax.broadcasted_iota(jnp.int32, (cols, channels), 0)
    left = jnp.where(position == 0, 0.0, pltpu.roll(wide, 1, 0))
    right = jnp.where(position == cols - 1, 0.0, pltpu.roll(wide, cols - 1, 0))
    target[row, :, 0:channels] = left.astype(jnp.bfloat16)
    target[row, :, channels : 2 * channels] = value
    target[row, :, 2 * channels : 3 * channels] = right.astype(jnp.bfloat16)


def halo_row(first, second, odd, row):
    one, other = first[row % 2], second[row % 2]
    return jnp.where(odd == (row < 2), one, other)


def fill(target, own, first, second, odd, base=0):
    for row in range(2):
        widen(target, row, halo_row(first, second, odd, row))
        widen(target, row + 2, own[base + row])
        widen(target, row + 4, halo_row(first, second, odd, row + 2))


def taps(source, start, rows):
    _, cols, width = source.shape
    return jnp.concatenate(
        [source[start + tap : start + tap + rows].reshape(rows * cols, width) for tap in range(3)],
        -1,
    )


def columns(weight, lo, channels, out_lo, out_hi):
    return weight[:, :, lo : lo + channels, out_lo:out_hi].reshape(9 * channels, out_hi - out_lo)


def product(left, right):
    return jnp.dot(left, right, preferred_element_type=jnp.float32)


def active(lag, layer):
    return layer == 0 if lag == 0 else layer == 1 if lag == 3 else layer >= 0


def is_odd():
    return lax.rem(lax.axis_index("rows"), 2) == 1


def pick_kernel(initial, frames, out, ready):
    layer = lax.axis_index("layer")
    for wanted, source in enumerate((initial, frames.at[0:2])):
        @pl.when(layer == wanted)
        def _():
            copy = pltpu.make_async_copy(source, out, ready)
            copy.start()
            copy.wait()


def stage_kernel(frames, weight, out, state_weight, ready):
    channels = weight.shape[2] // 2
    load = pltpu.make_async_copy(
        weight.at[:, :, channels : 2 * channels], state_weight, ready.at[0]
    )
    for wanted in range(2):
        @pl.when(lax.axis_index("layer") == wanted)
        def _():
            copy = pltpu.make_async_copy(
                frames.at[2 * wanted + 2 : 2 * wanted + 4], out, ready.at[1]
            )
            copy.start()
            load.start()
            copy.wait()
            load.wait()


def early_kernel(lag, own, first, second, wg, pre_r, pre_u, wide):
    cols, channels = own.shape[1:]

    @pl.when(active(lag, lax.axis_index("layer")))
    def _():
        fill(wide, own, first, second, is_odd())
        inner = product(taps(wide, 1, 2), columns(wg, 0, channels, 0, 2 * channels))
        edges = jnp.concatenate([taps(wide, 0, 1), taps(wide, 3, 1)], 0)
        outer = product(edges, columns(wg, 0, channels, channels, 2 * channels))
        pre_u[...] = inner[:, 0:channels]
        pre_r[cols : 3 * cols] = inner[:, channels : 2 * channels]
        pre_r[0:cols] = outer[0:cols]
        pre_r[3 * cols : 4 * cols] = outer[cols : 2 * cols]


def late_body(lag, own, first, second, pre, x0, x1, wg, wc, bias, wide, wide_r, store):
    cols, channels = own.shape[1:]
    layer, odd = lax.axis_index("layer"), is_odd()
    if lag < 3:
        @pl.when(layer == 0)
        def _():
            fill(wide, *x0, odd, 2 * lag)

    if lag > 0:
        @pl.when(layer == 1)
        def _():
            fill(wide, *x1, odd)

    of_reset = product(taps(wide, 0, 4), columns(wg, 0, channels, channels, 2 * channels))
    for row in range(4):
        part = slice(row * cols, (row + 1) * cols)
        held = own[row - 1] if 0 < row < 3 else halo_row(first, second, odd, 1 if row == 0 else 2)
        gate = jax.nn.sigmoid(
            pre[0][part] + of_reset[part] + bias[:, channels : 2 * channels]
        )
        widen(wide_r, row, (gate * held.astype(jnp.float32)).astype(jnp.bfloat16))
    weight = jnp.concatenate(
        [columns(wg, 0, channels, 0, channels), columns(wc, 0, channels, 0, channels)], -1
    )
    inner = product(taps(wide, 1, 2), weight)
    sum_u = pre[1][...] + inner[:, 0:channels]
    sum_c = inner[:, channels : 2 * channels] + product(
        taps(wide_r, 0, 2), columns(wc, channels, channels, 0, channels)
    )
    for row in range(2):
        part = slice(row * cols, (row + 1) * cols)
        held = own[row].astype(jnp.float32)
        update = jax.nn.sigmoid(sum_u[part] + bias[:, 0:channels])
        candidate = jnp.tanh(sum_c[part] + bias[:, 2 * channels : 3 * channels])
        store(row, ((1.0 - update) * held + update * candidate).astype(jnp.bfloat16))


def late_kernel(lag, *refs):
    own, first, second, pre_r, pre_u = refs[0:5]
    x0, x1 = refs[5:8], refs[8:11]
    wg, wc, bias, out, wide, wide_r = refs[11:17]

    def store(row, value):
        out[row] = value

    @pl.when(active(lag, lax.axis_index("layer")))
    def _():
        late_body(
            lag, own, first, second, (pre_r, pre_u), x0, x1, wg, wc, bias, wide, wide_r, store
        )

    if lag == 0:
        @pl.when(lax.axis_index("layer") == 1)
        def _():
            out[...] = own[...]


def last_kernel(*refs):
    own, first, second, pre_r, pre_u = refs[0:5]
    x1 = refs[5:8]
    wg, wc, bias, state0, state1, out, wide, wide_r, result, sent = refs[8:18]
    layer = lax.axis_index("layer")

    @pl.when(layer == 0)
    def _():
        copies = [
            pltpu.make_async_copy(state, out.at[frame], sent.at[frame])
            for frame, state in enumerate((state0, state1, own))
        ]
        for copy in copies:
            copy.start()
        for copy in copies:
            copy.wait()

    @pl.when(layer == 1)
    def _():
        copies = [
            pltpu.make_async_copy(state, out.at[frame], sent.at[frame])
            for frame, state in enumerate((state1, own))
        ]
        for copy in copies:
            copy.start()

        def store(row, value):
            result[row] = value
            copy = pltpu.make_async_copy(result.at[row], out.at[2, row], sent.at[2 + row])
            copy.start()
            copies.append(copy)

        late_body(
            3, own, first, second, (pre_r, pre_u), None, x1, wg, wc, bias, wide, wide_r, store
        )
        for copy in copies:
            copy.wait()


HELD = pl.BlockSpec(memory_space=pltpu.VMEM)
ANYWHERE = pl.BlockSpec(memory_space=pl.ANY)


def cost(units, cols, channels):
    return pl.CostEstimate(
        flops=2 * units * cols * channels * 9 * channels, bytes_accessed=1 << 20, transcendentals=0
    )


def wide_rows(rows, cols, channels):
    return pltpu.VMEM((rows, cols, 3 * channels), jnp.bfloat16)


def outside(array):
    return pltpu.with_memory_space_constraint(array, pltpu.HBM)


def pick(initial, rows):
    return pl.pallas_call(
        pick_kernel,
        out_shape=jax.ShapeDtypeStruct(initial.shape, initial.dtype),
        in_specs=[ANYWHERE] * 2,
        out_specs=HELD,
        scratch_shapes=[pltpu.SemaphoreType.DMA],
        compiler_params=pltpu.CompilerParams(vmem_limit_bytes=SMALL_BYTES),
    )(outside(initial), outside(rows))


def stage(rows, wg):
    _, cols, channels = rows.shape
    return pl.pallas_call(
        stage_kernel,
        out_shape=[
            jax.ShapeDtypeStruct((2, cols, channels), rows.dtype),
            jax.ShapeDtypeStruct((3, 3, channels, 2 * channels), wg.dtype),
        ],
        in_specs=[ANYWHERE] * 2,
        out_specs=[HELD] * 2,
        scratch_shapes=[pltpu.SemaphoreType.DMA((2,))],
        compiler_params=pltpu.CompilerParams(vmem_limit_bytes=SMALL_BYTES),
    )(outside(rows), outside(wg))


def early(lag, state, wg):
    _, cols, channels = state[0].shape
    pre = lambda n: jax.ShapeDtypeStruct((n * cols, channels), jnp.float32)
    return pl.pallas_call(
        functools.partial(early_kernel, lag),
        out_shape=[pre(4), pre(2)],
        in_specs=[HELD] * 4,
        out_specs=[HELD] * 2,
        scratch_shapes=[wide_rows(6, cols, channels)],
        compiler_params=pltpu.CompilerParams(vmem_limit_bytes=VMEM_BYTES),
        cost_estimate=cost(6, cols, channels),
    )(*state, wg)


def late(lag, state, pre, x0, x1, wg, wc, bias):
    _, cols, channels = state[0].shape
    return pl.pallas_call(
        functools.partial(late_kernel, lag),
        out_shape=jax.ShapeDtypeStruct((2, cols, channels), jnp.bfloat16),
        in_specs=[HELD] * 14,
        out_specs=HELD,
        scratch_shapes=[wide_rows(6, cols, channels), wide_rows(4, cols, channels)],
        compiler_params=pltpu.CompilerParams(vmem_limit_bytes=VMEM_BYTES),
        cost_estimate=cost(10, cols, channels),
    )(*state, *pre, *x0, *x1, wg, wc, bias)


def last(state, pre, x1, wg, wc, bias, earlier):
    _, cols, channels = state[0].shape
    return pl.pallas_call(
        last_kernel,
        out_shape=jax.ShapeDtypeStruct((3, 2, cols, channels), jnp.bfloat16),
        in_specs=[HELD] * 13,
        out_specs=ANYWHERE,
        scratch_shapes=[
            wide_rows(6, cols, channels),
            wide_rows(4, cols, channels),
            pltpu.VMEM((2, cols, channels), jnp.bfloat16),
            pltpu.SemaphoreType.DMA((4,)),
        ],
        compiler_params=pltpu.CompilerParams(vmem_limit_bytes=VMEM_BYTES),
        cost_estimate=cost(10, cols, channels),
    )(*state, *pre, *x1, wg, wc, bias, *earlier)


def pair_swap(field, start):
    count = lax.axis_size("rows")
    route = []
    for low in range(start, count - 1, 2):
        route += [(low, low + 1), (low + 1, low)]
    return lax.ppermute(field, "rows", route)


def gathered_swap(field, odd, inner):
    count = lax.axis_size("rows")
    groups = [[0, count], [count - 1, 2 * count - 1]]
    for layer in range(2):
        groups += [[layer * count + low, layer * count + low + 1] for low in range(1, count - 1, 2)]
    both = lax.all_gather(field, ("layer", "rows"), axis_index_groups=groups)
    partner = jnp.where(odd, both[1], both[0])
    return jnp.where(inner, partner, jnp.zeros_like(partner))


def across(field):
    return lax.ppermute(field, "layer", [(0, 1), (1, 0)])


def shards(frames, initial_state, w_gates, w_cand, biases):
    strip = lax.axis_index("rows")
    wg, wc = w_gates[0], w_cand[0]
    hidden = initial_state[0]
    rows = frames.reshape((6,) + hidden.shape[1:])

    odd = lax.rem(strip, 2) == 1
    inner = jnp.logical_and(strip > 0, strip < lax.axis_size("rows") - 1)
    field = pick(hidden, rows)
    field, odd, inner = lax.optimization_barrier((field, odd, inner))
    first, second = pair_swap(field, 0), pair_swap(field, 1)
    later_field, wg_state = stage(rows, wg)
    late_first, late_second = pair_swap(later_field, 0), pair_swap(later_field, 1)
    halos = [
        (across(first), across(second)),
        (late_first, late_second),
        (across(late_first), across(late_second)),
    ]
    below = (field, first, second)
    pre = early(0, below, wg_state)
    pre = lax.optimization_barrier((*pre, late_first, late_second))[0:2]
    hidden = late(0, (hidden, first, second), pre, (rows, *halos[0]), below, wg, wc, biases)
    states = [hidden]
    for step in range(1, 4):
        first = pair_swap(hidden, 0)
        own_below = across(hidden)
        second = gathered_swap(hidden, odd, inner)
        below = (own_below, across(first), across(second))
        state = (hidden, first, second)
        pre = early(step, state, wg_state)
        if step == 3:
            return last(state, pre, below, wg, wc, biases, states[0:2])[None]
        hidden = late(step, state, pre, (rows, *halos[step]), below, wg, wc, biases)
        states.append(hidden)


def solution(mesh):
    placed = (
        P(None, "rows", None, None),
        P("layer", "rows", None, None),
        P("layer", None, None, None, None),
        P("layer", None, None, None, None),
        P("layer", None),
    )
    return jax.shard_map(
        shards,
        mesh=mesh,
        in_specs=placed,
        out_specs=P("layer", None, "rows", None, None),
        check_vma=False,
    )
```

```python
import functools

import jax
import jax.numpy as jnp
from jax import lax
from jax.experimental import pallas as pl
from jax.experimental.pallas import tpu as pltpu
from jax.sharding import PartitionSpec as P

VMEM_BYTES = 16 * 1024 * 1024
SMALL_BYTES = 8 * 1024 * 1024


def widen(target, row, value):
    cols, channels = value.shape
    wide = value.astype(jnp.float32)
    position = lax.broadcasted_iota(jnp.int32, (cols, channels), 0)
    left = jnp.where(position == 0, 0.0, pltpu.roll(wide, 1, 0))
    right = jnp.where(position == cols - 1, 0.0, pltpu.roll(wide, cols - 1, 0))
    target[row, :, 0:channels] = left.astype(jnp.bfloat16)
    target[row, :, channels : 2 * channels] = value
    target[row, :, 2 * channels : 3 * channels] = right.astype(jnp.bfloat16)


def halo_row(first, second, odd, row):
    one, other = first[row % 2], second[row % 2]
    return jnp.where(odd == (row < 2), one, other)


def fill(target, own, first, second, odd, base=0):
    for row in range(2):
        widen(target, row, halo_row(first, second, odd, row))
        widen(target, row + 2, own[base + row])
        widen(target, row + 4, halo_row(first, second, odd, row + 2))


def taps(source, start, rows):
    _, cols, width = source.shape
    return jnp.concatenate(
        [source[start + tap : start + tap + rows].reshape(rows * cols, width) for tap in range(3)],
        -1,
    )


def columns(weight, lo, channels, out_lo, out_hi):
    return weight[:, :, lo : lo + channels, out_lo:out_hi].reshape(9 * channels, out_hi - out_lo)


def product(left, right):
    return jnp.dot(left, right, preferred_element_type=jnp.float32)


def active(lag, layer):
    return layer == 0 if lag == 0 else layer == 1 if lag == 3 else layer >= 0


def is_odd():
    return lax.rem(lax.axis_index("rows"), 2) == 1


def pick_kernel(initial, frames, out, later, ready):
    for wanted, sources in enumerate(
        ((initial, frames.at[2:4]), (frames.at[0:2], frames.at[4:6]))
    ):
        @pl.when(lax.axis_index("layer") == wanted)
        def _():
            copies = [
                pltpu.make_async_copy(source, target, ready.at[i])
                for i, (source, target) in enumerate(zip(sources, (out, later)))
            ]
            for copy in copies:
                copy.start()
            for copy in copies:
                copy.wait()


def stage_kernel(weight, state_weight, ready):
    channels = weight.shape[2] // 2
    load = pltpu.make_async_copy(weight.at[:, :, channels : 2 * channels], state_weight, ready)
    load.start()
    load.wait()


def early_kernel(lag, own, first, second, wg, pre_r, pre_u, wide):
    cols, channels = own.shape[1:]

    @pl.when(active(lag, lax.axis_index("layer")))
    def _():
        fill(wide, own, first, second, is_odd())
        inner = product(taps(wide, 1, 2), columns(wg, 0, channels, 0, 2 * channels))
        edges = jnp.concatenate([taps(wide, 0, 1), taps(wide, 3, 1)], 0)
        outer = product(edges, columns(wg, 0, channels, channels, 2 * channels))
        pre_u[...] = inner[:, 0:channels]
        pre_r[cols : 3 * cols] = inner[:, channels : 2 * channels]
        pre_r[0:cols] = outer[0:cols]
        pre_r[3 * cols : 4 * cols] = outer[cols : 2 * cols]


def late_body(lag, own, first, second, pre, x0, x1, wg, wc, bias, wide, wide_r, store):
    cols, channels = own.shape[1:]
    layer, odd = lax.axis_index("layer"), is_odd()
    if lag < 3:
        @pl.when(layer == 0)
        def _():
            fill(wide, *x0, odd, 2 * lag)

    if lag > 0:
        @pl.when(layer == 1)
        def _():
            fill(wide, *x1, odd)

    of_reset = product(taps(wide, 0, 4), columns(wg, 0, channels, channels, 2 * channels))
    for row in range(4):
        part = slice(row * cols, (row + 1) * cols)
        held = own[row - 1] if 0 < row < 3 else halo_row(first, second, odd, 1 if row == 0 else 2)
        gate = jax.nn.sigmoid(
            pre[0][part] + of_reset[part] + bias[:, channels : 2 * channels]
        )
        widen(wide_r, row, (gate * held.astype(jnp.float32)).astype(jnp.bfloat16))
    weight = jnp.concatenate(
        [columns(wg, 0, channels, 0, channels), columns(wc, 0, channels, 0, channels)], -1
    )
    inner = product(taps(wide, 1, 2), weight)
    sum_u = pre[1][...] + inner[:, 0:channels]
    sum_c = inner[:, channels : 2 * channels] + product(
        taps(wide_r, 0, 2), columns(wc, channels, channels, 0, channels)
    )
    for row in range(2):
        part = slice(row * cols, (row + 1) * cols)
        held = own[row].astype(jnp.float32)
        update = jax.nn.sigmoid(sum_u[part] + bias[:, 0:channels])
        candidate = jnp.tanh(sum_c[part] + bias[:, 2 * channels : 3 * channels])
        store(row, ((1.0 - update) * held + update * candidate).astype(jnp.bfloat16))


def late_kernel(lag, *refs):
    own, first, second, pre_r, pre_u = refs[0:5]
    x0, x1 = refs[5:8], refs[8:11]
    wg, wc, bias, out, wide, wide_r = refs[11:17]

    def store(row, value):
        out[row] = value

    @pl.when(active(lag, lax.axis_index("layer")))
    def _():
        late_body(
            lag, own, first, second, (pre_r, pre_u), x0, x1, wg, wc, bias, wide, wide_r, store
        )

    if lag == 0:
        @pl.when(lax.axis_index("layer") == 1)
        def _():
            out[...] = own[...]


def last_kernel(*refs):
    own, first, second, pre_r, pre_u = refs[0:5]
    x1 = refs[5:8]
    wg, wc, bias, state0, state1, out, wide, wide_r, result, sent = refs[8:18]
    layer = lax.axis_index("layer")

    @pl.when(layer == 0)
    def _():
        copies = [
            pltpu.make_async_copy(state, out.at[frame], sent.at[frame])
            for frame, state in enumerate((state0, state1, own))
        ]
        for copy in copies:
            copy.start()
        for copy in copies:
            copy.wait()

    @pl.when(layer == 1)
    def _():
        copies = [
            pltpu.make_async_copy(state, out.at[frame], sent.at[frame])
            for frame, state in enumerate((state1, own))
        ]
        for copy in copies:
            copy.start()

        def store(row, value):
            result[row] = value
            copy = pltpu.make_async_copy(result.at[row], out.at[2, row], sent.at[2 + row])
            copy.start()
            copies.append(copy)

        late_body(
            3, own, first, second, (pre_r, pre_u), None, x1, wg, wc, bias, wide, wide_r, store
        )
        for copy in copies:
            copy.wait()


HELD = pl.BlockSpec(memory_space=pltpu.VMEM)
ANYWHERE = pl.BlockSpec(memory_space=pl.ANY)


def cost(units, cols, channels):
    return pl.CostEstimate(
        flops=2 * units * cols * channels * 9 * channels, bytes_accessed=1 << 20, transcendentals=0
    )


def wide_rows(rows, cols, channels):
    return pltpu.VMEM((rows, cols, 3 * channels), jnp.bfloat16)


def outside(array):
    return pltpu.with_memory_space_constraint(array, pltpu.HBM)


def pick(initial, rows):
    return pl.pallas_call(
        pick_kernel,
        out_shape=[jax.ShapeDtypeStruct(initial.shape, initial.dtype)] * 2,
        in_specs=[ANYWHERE] * 2,
        out_specs=[HELD] * 2,
        scratch_shapes=[pltpu.SemaphoreType.DMA((2,))],
        compiler_params=pltpu.CompilerParams(vmem_limit_bytes=SMALL_BYTES),
    )(outside(initial), outside(rows))


def stage(wg):
    _, _, depth, width = wg.shape
    return pl.pallas_call(
        stage_kernel,
        out_shape=jax.ShapeDtypeStruct((3, 3, depth // 2, width), wg.dtype),
        in_specs=[ANYWHERE],
        out_specs=HELD,
        scratch_shapes=[pltpu.SemaphoreType.DMA],
        compiler_params=pltpu.CompilerParams(vmem_limit_bytes=SMALL_BYTES),
    )(outside(wg))


def early(lag, state, wg):
    _, cols, channels = state[0].shape
    pre = lambda n: jax.ShapeDtypeStruct((n * cols, channels), jnp.float32)
    return pl.pallas_call(
        functools.partial(early_kernel, lag),
        out_shape=[pre(4), pre(2)],
        in_specs=[HELD] * 4,
        out_specs=[HELD] * 2,
        scratch_shapes=[wide_rows(6, cols, channels)],
        compiler_params=pltpu.CompilerParams(vmem_limit_bytes=VMEM_BYTES),
        cost_estimate=cost(6, cols, channels),
    )(*state, wg)


def late(lag, state, pre, x0, x1, wg, wc, bias):
    _, cols, channels = state[0].shape
    return pl.pallas_call(
        functools.partial(late_kernel, lag),
        out_shape=jax.ShapeDtypeStruct((2, cols, channels), jnp.bfloat16),
        in_specs=[HELD] * 14,
        out_specs=HELD,
        scratch_shapes=[wide_rows(6, cols, channels), wide_rows(4, cols, channels)],
        compiler_params=pltpu.CompilerParams(vmem_limit_bytes=VMEM_BYTES),
        cost_estimate=cost(10, cols, channels),
    )(*state, *pre, *x0, *x1, wg, wc, bias)


def last(state, pre, x1, wg, wc, bias, earlier):
    _, cols, channels = state[0].shape
    return pl.pallas_call(
        last_kernel,
        out_shape=jax.ShapeDtypeStruct((3, 2, cols, channels), jnp.bfloat16),
        in_specs=[HELD] * 13,
        out_specs=ANYWHERE,
        scratch_shapes=[
            wide_rows(6, cols, channels),
            wide_rows(4, cols, channels),
            pltpu.VMEM((2, cols, channels), jnp.bfloat16),
            pltpu.SemaphoreType.DMA((4,)),
        ],
        compiler_params=pltpu.CompilerParams(vmem_limit_bytes=VMEM_BYTES),
        cost_estimate=cost(10, cols, channels),
    )(*state, *pre, *x1, wg, wc, bias, *earlier)


def pair_swap(field, start):
    count = lax.axis_size("rows")
    route = []
    for low in range(start, count - 1, 2):
        route += [(low, low + 1), (low + 1, low)]
    return lax.ppermute(field, "rows", route)


def gathered_swap(field, odd, inner, beside):
    count = lax.axis_size("rows")
    groups = [[0, count], [count - 1, 2 * count - 1]]
    for layer in range(2):
        groups += [[layer * count + low, layer * count + low + 1] for low in range(1, count - 1, 2)]
    both = lax.all_gather(field, ("layer", "rows"), axis_index_groups=groups)
    both, beside = lax.optimization_barrier((both, beside))
    partner = jnp.where(odd, both[1], both[0])
    return jnp.where(inner, partner, jnp.zeros_like(partner)), beside


def across(field):
    return lax.ppermute(field, "layer", [(0, 1), (1, 0)])


def shards(frames, initial_state, w_gates, w_cand, biases):
    strip = lax.axis_index("rows")
    wg, wc = w_gates[0], w_cand[0]
    hidden = initial_state[0]
    rows = frames.reshape((6,) + hidden.shape[1:])

    odd = lax.rem(strip, 2) == 1
    inner = jnp.logical_and(strip > 0, strip < lax.axis_size("rows") - 1)
    field, later_field = pick(hidden, rows)
    field, odd, inner = lax.optimization_barrier((field, odd, inner))
    first, second = pair_swap(field, 0), pair_swap(field, 1)
    wg_state = stage(wg)
    late_first, late_second = pair_swap(later_field, 0), pair_swap(later_field, 1)
    first_after, wg_state = lax.optimization_barrier((first, wg_state))
    halos = [
        (across(first_after), across(second)),
        (late_first, late_second),
        (across(late_first), across(late_second)),
    ]
    below = (field, first, second)
    pre = early(0, below, wg_state)
    pre = lax.optimization_barrier((*pre, late_first, late_second))[0:2]
    hidden = late(0, (hidden, first, second), pre, (rows, *halos[0]), below, wg, wc, biases)
    states = [hidden]
    for step in range(1, 4):
        first = pair_swap(hidden, 0)
        own_below = across(hidden)
        second, own_below = gathered_swap(hidden, odd, inner, own_below)
        below = (own_below, across(first), across(second))
        state = (hidden, first, second)
        pre = early(step, state, wg_state)
        if step == 3:
            return last(state, pre, below, wg, wc, biases, states[0:2])[None]
        hidden = late(step, state, pre, (rows, *halos[step]), below, wg, wc, biases)
        states.append(hidden)


def solution(mesh):
    placed = (
        P(None, "rows", None, None),
        P("layer", "rows", None, None),
        P("layer", None, None, None, None),
        P("layer", None, None, None, None),
        P("layer", None),
    )
    return jax.shard_map(
        shards,
        mesh=mesh,
        in_specs=placed,
        out_specs=P("layer", None, "rows", None, None),
        check_vma=False,
    )
```

```python
import functools

import jax
import jax.numpy as jnp
from jax import lax
from jax.experimental import pallas as pl
from jax.experimental.pallas import tpu as pltpu
from jax.sharding import PartitionSpec as P

VMEM_BYTES = 16 * 1024 * 1024
SMALL_BYTES = 8 * 1024 * 1024


def widen(target, row, value):
    cols, channels = value.shape
    wide = value.astype(jnp.float32)
    position = lax.broadcasted_iota(jnp.int32, (cols, channels), 0)
    left = jnp.where(position == 0, 0.0, pltpu.roll(wide, 1, 0))
    right = jnp.where(position == cols - 1, 0.0, pltpu.roll(wide, cols - 1, 0))
    target[row, :, 0:channels] = left.astype(jnp.bfloat16)
    target[row, :, channels : 2 * channels] = value
    target[row, :, 2 * channels : 3 * channels] = right.astype(jnp.bfloat16)


def halo_row(first, second, odd, row):
    one, other = first[row % 2], second[row % 2]
    return jnp.where(odd == (row < 2), one, other)


def spread(own, first, second, base=0):
    odd = is_odd()
    return (
        [functools.partial(halo_row, first, second, odd, row) for row in range(2)]
        + [functools.partial(lambda row: own[base + row], row) for row in range(2)]
        + [functools.partial(halo_row, first, second, odd, row) for row in range(2, 4)]
    )


def fill(target, rows):
    for row, value in enumerate(rows):
        widen(target, row, value())


def taps(source, start, rows):
    _, cols, width = source.shape
    return jnp.concatenate(
        [source[start + tap : start + tap + rows].reshape(rows * cols, width) for tap in range(3)],
        -1,
    )


def columns(weight, lo, channels, out_lo, out_hi):
    return weight[:, :, lo : lo + channels, out_lo:out_hi].reshape(9 * channels, out_hi - out_lo)


def product(left, right):
    return jnp.dot(left, right, preferred_element_type=jnp.float32)


def where_active(lag, work):
    if lag in (0, 3):
        pl.when(lax.axis_index("layer") == (0 if lag == 0 else 1))(work)
    else:
        work()


def is_odd():
    return lax.rem(lax.axis_index("rows"), 2) == 1


def pick_kernel(initial, frames, out, later, ready):
    for wanted, sources in enumerate(
        ((initial, frames.at[2:4]), (frames.at[0:2], frames.at[4:6]))
    ):
        @pl.when(lax.axis_index("layer") == wanted)
        def _():
            copies = [
                pltpu.make_async_copy(source, target, ready.at[i])
                for i, (source, target) in enumerate(zip(sources, (out, later)))
            ]
            for copy in copies:
                copy.start()
            for copy in copies:
                copy.wait()


def stage_kernel(weight, state_weight, ready):
    channels = weight.shape[2] // 2
    load = pltpu.make_async_copy(weight.at[:, :, channels : 2 * channels], state_weight, ready)
    load.start()
    load.wait()


def early_kernel(lag, own, first, second, wg, pre_r, pre_u, wide):
    cols, channels = own.shape[1:]

    def work():
        fill(wide, spread(own, first, second))
        inner = product(taps(wide, 1, 2), columns(wg, 0, channels, 0, 2 * channels))
        edges = jnp.concatenate([taps(wide, 0, 1), taps(wide, 3, 1)], 0)
        outer = product(edges, columns(wg, 0, channels, channels, 2 * channels))
        pre_u[...] = inner[:, 0:channels]
        pre_r[cols : 3 * cols] = inner[:, channels : 2 * channels]
        pre_r[0:cols] = outer[0:cols]
        pre_r[3 * cols : 4 * cols] = outer[cols : 2 * cols]

    where_active(lag, work)


def late_body(lag, own, first, second, pre, x0, x1, wg, wc, bias, wide, wide_r, store):
    cols, channels = own.shape[1:]
    odd = is_odd()
    if lag == 0:
        fill(wide, spread(*x0))
    elif lag == 3:
        fill(wide, spread(*x1))
    else:
        lower = lax.axis_index("layer") == 0
        for row, (one, other) in enumerate(zip(spread(*x0, 2 * lag), spread(*x1))):
            widen(wide, row, jnp.where(lower, one(), other()))

    of_reset = product(taps(wide, 0, 4), columns(wg, 0, channels, channels, 2 * channels))
    for row in range(4):
        part = slice(row * cols, (row + 1) * cols)
        held = own[row - 1] if 0 < row < 3 else halo_row(first, second, odd, 1 if row == 0 else 2)
        gate = jax.nn.sigmoid(
            pre[0][part] + of_reset[part] + bias[:, channels : 2 * channels]
        )
        widen(wide_r, row, (gate * held.astype(jnp.float32)).astype(jnp.bfloat16))
    weight = jnp.concatenate(
        [columns(wg, 0, channels, 0, channels), columns(wc, 0, channels, 0, channels)], -1
    )
    inner = product(taps(wide, 1, 2), weight)
    sum_u = pre[1][...] + inner[:, 0:channels]
    sum_c = inner[:, channels : 2 * channels] + product(
        taps(wide_r, 0, 2), columns(wc, channels, channels, 0, channels)
    )
    for row in range(2):
        part = slice(row * cols, (row + 1) * cols)
        held = own[row].astype(jnp.float32)
        update = jax.nn.sigmoid(sum_u[part] + bias[:, 0:channels])
        candidate = jnp.tanh(sum_c[part] + bias[:, 2 * channels : 3 * channels])
        store(row, ((1.0 - update) * held + update * candidate).astype(jnp.bfloat16))


def late_kernel(lag, *refs):
    own, first, second, pre_r, pre_u = refs[0:5]
    x0, x1 = refs[5:8], refs[8:11]
    wg, wc, bias, out, wide, wide_r = refs[11:17]

    def store(row, value):
        out[row] = value

    def work():
        late_body(
            lag, own, first, second, (pre_r, pre_u), x0, x1, wg, wc, bias, wide, wide_r, store
        )

    where_active(lag, work)
    if lag == 0:
        @pl.when(lax.axis_index("layer") == 1)
        def _():
            out[...] = own[...]


def last_kernel(*refs):
    own, first, second, pre_r, pre_u = refs[0:5]
    x1 = refs[5:8]
    wg, wc, bias, state0, state1, out, wide, wide_r, result, sent = refs[8:18]
    layer = lax.axis_index("layer")

    @pl.when(layer == 0)
    def _():
        copies = [
            pltpu.make_async_copy(state, out.at[frame], sent.at[frame])
            for frame, state in enumerate((state0, state1, own))
        ]
        for copy in copies:
            copy.start()
        for copy in copies:
            copy.wait()

    @pl.when(layer == 1)
    def _():
        copies = [
            pltpu.make_async_copy(state, out.at[frame], sent.at[frame])
            for frame, state in enumerate((state1, own))
        ]
        for copy in copies:
            copy.start()

        def store(row, value):
            result[row] = value
            copy = pltpu.make_async_copy(result.at[row], out.at[2, row], sent.at[2 + row])
            copy.start()
            copies.append(copy)

        late_body(
            3, own, first, second, (pre_r, pre_u), None, x1, wg, wc, bias, wide, wide_r, store
        )
        for copy in copies:
            copy.wait()


HELD = pl.BlockSpec(memory_space=pltpu.VMEM)
ANYWHERE = pl.BlockSpec(memory_space=pl.ANY)


def cost(units, cols, channels):
    return pl.CostEstimate(
        flops=2 * units * cols * channels * 9 * channels, bytes_accessed=1 << 20, transcendentals=0
    )


def wide_rows(rows, cols, channels):
    return pltpu.VMEM((rows, cols, 3 * channels), jnp.bfloat16)


def outside(array):
    return pltpu.with_memory_space_constraint(array, pltpu.HBM)


def pick(initial, rows):
    return pl.pallas_call(
        pick_kernel,
        out_shape=[jax.ShapeDtypeStruct(initial.shape, initial.dtype)] * 2,
        in_specs=[ANYWHERE] * 2,
        out_specs=[HELD] * 2,
        scratch_shapes=[pltpu.SemaphoreType.DMA((2,))],
        compiler_params=pltpu.CompilerParams(vmem_limit_bytes=SMALL_BYTES),
    )(outside(initial), outside(rows))


def stage(wg):
    _, _, depth, width = wg.shape
    return pl.pallas_call(
        stage_kernel,
        out_shape=jax.ShapeDtypeStruct((3, 3, depth // 2, width), wg.dtype),
        in_specs=[ANYWHERE],
        out_specs=HELD,
        scratch_shapes=[pltpu.SemaphoreType.DMA],
        compiler_params=pltpu.CompilerParams(vmem_limit_bytes=SMALL_BYTES),
    )(outside(wg))


def early(lag, state, wg):
    _, cols, channels = state[0].shape
    pre = lambda n: jax.ShapeDtypeStruct((n * cols, channels), jnp.float32)
    return pl.pallas_call(
        functools.partial(early_kernel, lag),
        out_shape=[pre(4), pre(2)],
        in_specs=[HELD] * 4,
        out_specs=[HELD] * 2,
        scratch_shapes=[wide_rows(6, cols, channels)],
        compiler_params=pltpu.CompilerParams(vmem_limit_bytes=VMEM_BYTES),
        cost_estimate=cost(6, cols, channels),
    )(*state, wg)


def late(lag, state, pre, x0, x1, wg, wc, bias):
    _, cols, channels = state[0].shape
    return pl.pallas_call(
        functools.partial(late_kernel, lag),
        out_shape=jax.ShapeDtypeStruct((2, cols, channels), jnp.bfloat16),
        in_specs=[HELD] * 14,
        out_specs=HELD,
        scratch_shapes=[wide_rows(6, cols, channels), wide_rows(4, cols, channels)],
        compiler_params=pltpu.CompilerParams(vmem_limit_bytes=VMEM_BYTES),
        cost_estimate=cost(10, cols, channels),
    )(*state, *pre, *x0, *x1, wg, wc, bias)


def last(state, pre, x1, wg, wc, bias, earlier):
    _, cols, channels = state[0].shape
    return pl.pallas_call(
        last_kernel,
        out_shape=jax.ShapeDtypeStruct((3, 2, cols, channels), jnp.bfloat16),
        in_specs=[HELD] * 13,
        out_specs=ANYWHERE,
        scratch_shapes=[
            wide_rows(6, cols, channels),
            wide_rows(4, cols, channels),
            pltpu.VMEM((2, cols, channels), jnp.bfloat16),
            pltpu.SemaphoreType.DMA((4,)),
        ],
        compiler_params=pltpu.CompilerParams(vmem_limit_bytes=VMEM_BYTES),
        cost_estimate=cost(10, cols, channels),
    )(*state, *pre, *x1, wg, wc, bias, *earlier)


def pair_swap(field, start):
    count = lax.axis_size("rows")
    route = []
    for low in range(start, count - 1, 2):
        route += [(low, low + 1), (low + 1, low)]
    return lax.ppermute(field, "rows", route)


def gathered_swap(field, odd, inner, beside):
    count = lax.axis_size("rows")
    groups = [[0, count], [count - 1, 2 * count - 1]]
    for layer in range(2):
        groups += [[layer * count + low, layer * count + low + 1] for low in range(1, count - 1, 2)]
    both = lax.all_gather(field, ("layer", "rows"), axis_index_groups=groups)
    if beside is not None:
        both, beside = lax.optimization_barrier((both, beside))
    partner = jnp.where(odd, both[1], both[0])
    return jnp.where(inner, partner, jnp.zeros_like(partner)), beside


def across(field):
    return lax.ppermute(field, "layer", [(0, 1), (1, 0)])


def shards(frames, initial_state, w_gates, w_cand, biases):
    strip = lax.axis_index("rows")
    wg, wc = w_gates[0], w_cand[0]
    hidden = initial_state[0]
    rows = frames.reshape((6,) + hidden.shape[1:])

    odd = lax.rem(strip, 2) == 1
    inner = jnp.logical_and(strip > 0, strip < lax.axis_size("rows") - 1)
    field, later_field = pick(hidden, rows)
    field, odd, inner = lax.optimization_barrier((field, odd, inner))
    first, second = pair_swap(field, 0), pair_swap(field, 1)
    wg_state = stage(wg)
    late_first, late_second = pair_swap(later_field, 0), pair_swap(later_field, 1)
    first_after, wg_state = lax.optimization_barrier((first, wg_state))
    halos = [
        (across(first_after), across(second)),
        (late_first, late_second),
        (across(late_first), across(late_second)),
    ]
    below = (field, first, second)
    pre = early(0, below, wg_state)
    pre = lax.optimization_barrier((*pre, late_first, late_second))[0:2]
    hidden = late(0, (hidden, first, second), pre, (rows, *halos[0]), below, wg, wc, biases)
    states = [hidden]
    for step in range(1, 4):
        first = pair_swap(hidden, 0)
        own_below = across(hidden)
        second, waited = gathered_swap(hidden, odd, inner, own_below if step > 1 else None)
        own_below = waited if step > 1 else own_below
        below = (own_below, across(first), across(second))
        state = (hidden, first, second)
        pre = early(step, state, wg_state)
        if step == 3:
            return last(state, pre, below, wg, wc, biases, states[0:2])[None]
        hidden = late(step, state, pre, (rows, *halos[step]), below, wg, wc, biases)
        states.append(hidden)


def solution(mesh):
    placed = (
        P(None, "rows", None, None),
        P("layer", "rows", None, None),
        P("layer", None, None, None, None),
        P("layer", None, None, None, None),
        P("layer", None),
    )
    return jax.shard_map(
        shards,
        mesh=mesh,
        in_specs=placed,
        out_specs=P("layer", None, "rows", None, None),
        check_vma=False,
    )
```

```python
import functools

import jax
import jax.numpy as jnp
from jax import lax
from jax.experimental import pallas as pl
from jax.experimental.pallas import tpu as pltpu
from jax.sharding import PartitionSpec as P

VMEM_BYTES = 16 * 1024 * 1024
SMALL_BYTES = 8 * 1024 * 1024


def widen(target, row, value):
    cols, channels = value.shape
    wide = value.astype(jnp.float32)
    position = lax.broadcasted_iota(jnp.int32, (cols, channels), 0)
    left = jnp.where(position == 0, 0.0, pltpu.roll(wide, 1, 0))
    right = jnp.where(position == cols - 1, 0.0, pltpu.roll(wide, cols - 1, 0))
    target[row, :, 0:channels] = left.astype(jnp.bfloat16)
    target[row, :, channels : 2 * channels] = value
    target[row, :, 2 * channels : 3 * channels] = right.astype(jnp.bfloat16)


def halo_row(first, second, odd, row):
    one, other = first[row % 2], second[row % 2]
    return jnp.where(odd == (row < 2), one, other)


def spread(own, first, second, base=0):
    odd = is_odd()
    return (
        [functools.partial(halo_row, first, second, odd, row) for row in range(2)]
        + [functools.partial(lambda row: own[base + row], row) for row in range(2)]
        + [functools.partial(halo_row, first, second, odd, row) for row in range(2, 4)]
    )


def fill(target, rows):
    for row, value in enumerate(rows):
        widen(target, row, value())


def taps(source, start, rows):
    _, cols, width = source.shape
    return jnp.concatenate(
        [source[start + tap : start + tap + rows].reshape(rows * cols, width) for tap in range(3)],
        -1,
    )


def columns(weight, lo, channels, out_lo, out_hi):
    return weight[:, :, lo : lo + channels, out_lo:out_hi].reshape(9 * channels, out_hi - out_lo)


def product(left, right):
    return jnp.dot(left, right, preferred_element_type=jnp.float32)


def where_active(lag, work):
    if lag in (0, 3):
        pl.when(lax.axis_index("layer") == (0 if lag == 0 else 1))(work)
    else:
        work()


def is_odd():
    return lax.rem(lax.axis_index("rows"), 2) == 1


def pick_kernel(initial, frames, out, later, ready):
    for wanted, sources in enumerate(
        ((initial, frames.at[2:4]), (frames.at[0:2], frames.at[4:6]))
    ):
        @pl.when(lax.axis_index("layer") == wanted)
        def _():
            copies = [
                pltpu.make_async_copy(source, target, ready.at[i])
                for i, (source, target) in enumerate(zip(sources, (out, later)))
            ]
            for copy in copies:
                copy.start()
            for copy in copies:
                copy.wait()


def stage_kernel(weight, state_weight, ready):
    channels = weight.shape[2] // 2
    load = pltpu.make_async_copy(weight.at[:, :, channels : 2 * channels], state_weight, ready)
    load.start()
    load.wait()


def early_kernel(lag, own, first, second, wg, pre_r, pre_u, wide):
    cols, channels = own.shape[1:]

    def work():
        fill(wide, spread(own, first, second))
        inner = product(taps(wide, 1, 2), columns(wg, 0, channels, 0, 2 * channels))
        edges = jnp.concatenate([taps(wide, 0, 1), taps(wide, 3, 1)], 0)
        outer = product(edges, columns(wg, 0, channels, channels, 2 * channels))
        pre_u[...] = inner[:, 0:channels]
        pre_r[cols : 3 * cols] = inner[:, channels : 2 * channels]
        pre_r[0:cols] = outer[0:cols]
        pre_r[3 * cols : 4 * cols] = outer[cols : 2 * cols]

    where_active(lag, work)


def late_body(lag, own, first, second, pre, x0, x1, wg, wc, bias, wide, wide_r, store):
    cols, channels = own.shape[1:]
    odd = is_odd()
    if lag == 0:
        fill(wide, spread(*x0))
    elif lag == 3:
        fill(wide, spread(*x1))
    else:
        lower = lax.axis_index("layer") == 0
        for row, (one, other) in enumerate(zip(spread(*x0, 2 * lag), spread(*x1))):
            widen(wide, row, jnp.where(lower, one(), other()))

    of_reset = product(taps(wide, 0, 4), columns(wg, 0, channels, channels, 2 * channels))
    for row in range(4):
        part = slice(row * cols, (row + 1) * cols)
        held = own[row - 1] if 0 < row < 3 else halo_row(first, second, odd, 1 if row == 0 else 2)
        gate = jax.nn.sigmoid(
            pre[0][part] + of_reset[part] + bias[:, channels : 2 * channels]
        )
        widen(wide_r, row, (gate * held.astype(jnp.float32)).astype(jnp.bfloat16))
    weight = jnp.concatenate(
        [columns(wg, 0, channels, 0, channels), columns(wc, 0, channels, 0, channels)], -1
    )
    inner = product(taps(wide, 1, 2), weight)
    sum_u = pre[1][...] + inner[:, 0:channels]
    sum_c = inner[:, channels : 2 * channels] + product(
        taps(wide_r, 0, 2), columns(wc, channels, channels, 0, channels)
    )
    for row in range(2):
        part = slice(row * cols, (row + 1) * cols)
        held = own[row].astype(jnp.float32)
        update = jax.nn.sigmoid(sum_u[part] + bias[:, 0:channels])
        candidate = jnp.tanh(sum_c[part] + bias[:, 2 * channels : 3 * channels])
        store(row, ((1.0 - update) * held + update * candidate).astype(jnp.bfloat16))


def late_kernel(lag, *refs):
    own, first, second, pre_r, pre_u = refs[0:5]
    x0, x1 = refs[5:8], refs[8:11]
    wg, wc, bias, out, wide, wide_r = refs[11:17]

    def store(row, value):
        out[row] = value

    def work():
        late_body(
            lag, own, first, second, (pre_r, pre_u), x0, x1, wg, wc, bias, wide, wide_r, store
        )

    where_active(lag, work)
    if lag == 0:
        @pl.when(lax.axis_index("layer") == 1)
        def _():
            out[...] = own[...]


def last_kernel(*refs):
    own, first, second, pre_r, pre_u = refs[0:5]
    x1 = refs[5:8]
    wg, wc, bias, state0, state1, out, wide, wide_r, result, sent = refs[8:18]
    layer = lax.axis_index("layer")

    @pl.when(layer == 0)
    def _():
        copies = [
            pltpu.make_async_copy(state, out.at[frame], sent.at[frame])
            for frame, state in enumerate((state0, state1, own))
        ]
        for copy in copies:
            copy.start()
        for copy in copies:
            copy.wait()

    @pl.when(layer == 1)
    def _():
        copies = [
            pltpu.make_async_copy(state, out.at[frame], sent.at[frame])
            for frame, state in enumerate((state1, own))
        ]
        for copy in copies:
            copy.start()

        def store(row, value):
            result[row] = value
            copy = pltpu.make_async_copy(result.at[row], out.at[2, row], sent.at[2 + row])
            copy.start()
            copies.append(copy)

        late_body(
            3, own, first, second, (pre_r, pre_u), None, x1, wg, wc, bias, wide, wide_r, store
        )
        for copy in copies:
            copy.wait()


HELD = pl.BlockSpec(memory_space=pltpu.VMEM)
ANYWHERE = pl.BlockSpec(memory_space=pl.ANY)


def cost(units, cols, channels):
    return pl.CostEstimate(
        flops=2 * units * cols * channels * 9 * channels, bytes_accessed=1 << 20, transcendentals=0
    )


def wide_rows(rows, cols, channels):
    return pltpu.VMEM((rows, cols, 3 * channels), jnp.bfloat16)


def outside(array):
    return pltpu.with_memory_space_constraint(array, pltpu.HBM)


def pick(initial, rows):
    return pl.pallas_call(
        pick_kernel,
        out_shape=[jax.ShapeDtypeStruct(initial.shape, initial.dtype)] * 2,
        in_specs=[ANYWHERE] * 2,
        out_specs=[HELD] * 2,
        scratch_shapes=[pltpu.SemaphoreType.DMA((2,))],
        compiler_params=pltpu.CompilerParams(vmem_limit_bytes=SMALL_BYTES),
    )(outside(initial), outside(rows))


def stage(wg):
    _, _, depth, width = wg.shape
    return pl.pallas_call(
        stage_kernel,
        out_shape=jax.ShapeDtypeStruct((3, 3, depth // 2, width), wg.dtype),
        in_specs=[ANYWHERE],
        out_specs=HELD,
        scratch_shapes=[pltpu.SemaphoreType.DMA],
        compiler_params=pltpu.CompilerParams(vmem_limit_bytes=SMALL_BYTES),
    )(outside(wg))


def early(lag, state, wg):
    _, cols, channels = state[0].shape
    pre = lambda n: jax.ShapeDtypeStruct((n * cols, channels), jnp.float32)
    return pl.pallas_call(
        functools.partial(early_kernel, lag),
        out_shape=[pre(4), pre(2)],
        in_specs=[HELD] * 4,
        out_specs=[HELD] * 2,
        scratch_shapes=[wide_rows(6, cols, channels)],
        compiler_params=pltpu.CompilerParams(vmem_limit_bytes=VMEM_BYTES),
        cost_estimate=cost(6, cols, channels),
    )(*state, wg)


def late(lag, state, pre, x0, x1, wg, wc, bias):
    _, cols, channels = state[0].shape
    return pl.pallas_call(
        functools.partial(late_kernel, lag),
        out_shape=jax.ShapeDtypeStruct((2, cols, channels), jnp.bfloat16),
        in_specs=[HELD] * 14,
        out_specs=HELD,
        scratch_shapes=[wide_rows(6, cols, channels), wide_rows(4, cols, channels)],
        compiler_params=pltpu.CompilerParams(vmem_limit_bytes=VMEM_BYTES),
        cost_estimate=cost(10, cols, channels),
    )(*state, *pre, *x0, *x1, wg, wc, bias)


def last(state, pre, x1, wg, wc, bias, earlier):
    _, cols, channels = state[0].shape
    return pl.pallas_call(
        last_kernel,
        out_shape=jax.ShapeDtypeStruct((3, 2, cols, channels), jnp.bfloat16),
        in_specs=[HELD] * 13,
        out_specs=ANYWHERE,
        scratch_shapes=[
            wide_rows(6, cols, channels),
            wide_rows(4, cols, channels),
            pltpu.VMEM((2, cols, channels), jnp.bfloat16),
            pltpu.SemaphoreType.DMA((4,)),
        ],
        compiler_params=pltpu.CompilerParams(vmem_limit_bytes=VMEM_BYTES),
        cost_estimate=cost(10, cols, channels),
    )(*state, *pre, *x1, wg, wc, bias, *earlier)


def pair_swap(field, start):
    count = lax.axis_size("rows")
    route = []
    for low in range(start, count - 1, 2):
        route += [(low, low + 1), (low + 1, low)]
    return lax.ppermute(field, "rows", route)


def gathered_swap(field, odd, inner, beside):
    count = lax.axis_size("rows")
    groups = [[0, count], [count - 1, 2 * count - 1]]
    for layer in range(2):
        groups += [[layer * count + low, layer * count + low + 1] for low in range(1, count - 1, 2)]
    both = lax.all_gather(field, ("layer", "rows"), axis_index_groups=groups)
    if beside is not None:
        both, beside = lax.optimization_barrier((both, beside))
    partner = jnp.where(odd, both[1], both[0])
    return jnp.where(inner, partner, jnp.zeros_like(partner)), beside


def across(field):
    return lax.ppermute(field, "layer", [(0, 1), (1, 0)])


def shards(frames, initial_state, w_gates, w_cand, biases):
    strip = lax.axis_index("rows")
    wg, wc = w_gates[0], w_cand[0]
    hidden = initial_state[0]
    rows = frames.reshape((6,) + hidden.shape[1:])

    odd = lax.rem(strip, 2) == 1
    inner = jnp.logical_and(strip > 0, strip < lax.axis_size("rows") - 1)
    field, later_field = pick(hidden, rows)
    field, odd, inner = lax.optimization_barrier((field, odd, inner))
    second = pair_swap(field, 1)
    first = pair_swap(field, 0)
    wg_state = stage(wg)
    late_second = pair_swap(later_field, 1)
    late_first = pair_swap(later_field, 0)
    second_after, wg_state = lax.optimization_barrier((second, wg_state))
    halos = [
        (across(first), across(second_after)),
        (late_first, late_second),
        (across(late_first), across(late_second)),
    ]
    below = (field, first, second)
    pre = early(0, below, wg_state)
    pre = lax.optimization_barrier((*pre, late_second, late_first))[0:2]
    hidden = late(0, (hidden, first, second), pre, (rows, *halos[0]), below, wg, wc, biases)
    states = [hidden]
    for step in range(1, 4):
        first = pair_swap(hidden, 0)
        own_below = across(hidden)
        second, waited = gathered_swap(hidden, odd, inner, own_below if step > 1 else None)
        own_below = waited if step > 1 else own_below
        below = (own_below, across(first), across(second))
        state = (hidden, first, second)
        pre = early(step, state, wg_state)
        if step == 3:
            return last(state, pre, below, wg, wc, biases, states[0:2])[None]
        hidden = late(step, state, pre, (rows, *halos[step]), below, wg, wc, biases)
        states.append(hidden)


def solution(mesh):
    placed = (
        P(None, "rows", None, None),
        P("layer", "rows", None, None),
        P("layer", None, None, None, None),
        P("layer", None, None, None, None),
        P("layer", None),
    )
    return jax.shard_map(
        shards,
        mesh=mesh,
        in_specs=placed,
        out_specs=P("layer", None, "rows", None, None),
        check_vma=False,
    )
```

```python
import functools

import jax
import jax.numpy as jnp
from jax import lax
from jax.experimental import pallas as pl
from jax.experimental.pallas import tpu as pltpu
from jax.sharding import PartitionSpec as P

VMEM_BYTES = 16 * 1024 * 1024
SMALL_BYTES = 8 * 1024 * 1024


def widen(target, row, value):
    cols, channels = value.shape
    wide = value.astype(jnp.float32)
    position = lax.broadcasted_iota(jnp.int32, (cols, channels), 0)
    left = jnp.where(position == 0, 0.0, pltpu.roll(wide, 1, 0))
    right = jnp.where(position == cols - 1, 0.0, pltpu.roll(wide, cols - 1, 0))
    target[row, :, 0:channels] = left.astype(jnp.bfloat16)
    target[row, :, channels : 2 * channels] = value
    target[row, :, 2 * channels : 3 * channels] = right.astype(jnp.bfloat16)


def halo_row(first, second, odd, row):
    one, other = first[row % 2], second[row % 2]
    return jnp.where(odd == (row < 2), one, other)


def spread(own, first, second, base=0):
    odd = is_odd()
    return (
        [functools.partial(halo_row, first, second, odd, row) for row in range(2)]
        + [functools.partial(lambda row: own[base + row], row) for row in range(2)]
        + [functools.partial(halo_row, first, second, odd, row) for row in range(2, 4)]
    )


def fill(target, rows):
    for row, value in enumerate(rows):
        widen(target, row, value())


def taps(source, start, rows):
    _, cols, width = source.shape
    return jnp.concatenate(
        [source[start + tap : start + tap + rows].reshape(rows * cols, width) for tap in range(3)],
        -1,
    )


def columns(weight, lo, channels, out_lo, out_hi):
    return weight[:, :, lo : lo + channels, out_lo:out_hi].reshape(9 * channels, out_hi - out_lo)


def product(left, right):
    return jnp.dot(left, right, preferred_element_type=jnp.float32)


def where_active(lag, work):
    if lag in (0, 3):
        pl.when(lax.axis_index("layer") == (0 if lag == 0 else 1))(work)
    else:
        work()


def is_odd():
    return lax.rem(lax.axis_index("rows"), 2) == 1


def pick_kernel(initial, frames, out, later, ready):
    for wanted, sources in enumerate(
        ((initial, frames.at[2:4]), (frames.at[0:2], frames.at[4:6]))
    ):
        @pl.when(lax.axis_index("layer") == wanted)
        def _():
            copies = [
                pltpu.make_async_copy(source, target, ready.at[i])
                for i, (source, target) in enumerate(zip(sources, (out, later)))
            ]
            for copy in copies:
                copy.start()
            for copy in copies:
                copy.wait()


def stage_kernel(weight, state_weight, ready):
    channels = weight.shape[2] // 2
    load = pltpu.make_async_copy(weight.at[:, :, channels : 2 * channels], state_weight, ready)
    load.start()
    load.wait()


def early_kernel(lag, own, first, second, wg, pre_r, pre_u, wide):
    cols, channels = own.shape[1:]

    def work():
        fill(wide, spread(own, first, second))
        inner = product(taps(wide, 1, 2), columns(wg, 0, channels, 0, 2 * channels))
        edges = jnp.concatenate([taps(wide, 0, 1), taps(wide, 3, 1)], 0)
        outer = product(edges, columns(wg, 0, channels, channels, 2 * channels))
        pre_u[...] = inner[:, 0:channels]
        pre_r[cols : 3 * cols] = inner[:, channels : 2 * channels]
        pre_r[0:cols] = outer[0:cols]
        pre_r[3 * cols : 4 * cols] = outer[cols : 2 * cols]

    where_active(lag, work)


def late_body(lag, own, first, second, pre, x0, x1, wg, wc, bias, wide, wide_r, store):
    cols, channels = own.shape[1:]
    odd = is_odd()
    if lag == 0:
        fill(wide, spread(*x0))
    elif lag == 3:
        fill(wide, spread(*x1))
    else:
        lower = lax.axis_index("layer") == 0
        for row, (one, other) in enumerate(zip(spread(*x0, 2 * lag), spread(*x1))):
            widen(wide, row, jnp.where(lower, one(), other()))

    of_reset = product(taps(wide, 0, 4), columns(wg, 0, channels, channels, 2 * channels))
    for row in range(4):
        part = slice(row * cols, (row + 1) * cols)
        held = own[row - 1] if 0 < row < 3 else halo_row(first, second, odd, 1 if row == 0 else 2)
        gate = jax.nn.sigmoid(
            pre[0][part] + of_reset[part] + bias[:, channels : 2 * channels]
        )
        widen(wide_r, row, (gate * held.astype(jnp.float32)).astype(jnp.bfloat16))
    weight = jnp.concatenate(
        [columns(wg, 0, channels, 0, channels), columns(wc, 0, channels, 0, channels)], -1
    )
    inner = product(taps(wide, 1, 2), weight)
    sum_u = pre[1][...] + inner[:, 0:channels]
    sum_c = inner[:, channels : 2 * channels] + product(
        taps(wide_r, 0, 2), columns(wc, channels, channels, 0, channels)
    )
    for row in range(2):
        part = slice(row * cols, (row + 1) * cols)
        held = own[row].astype(jnp.float32)
        update = jax.nn.sigmoid(sum_u[part] + bias[:, 0:channels])
        candidate = jnp.tanh(sum_c[part] + bias[:, 2 * channels : 3 * channels])
        store(row, ((1.0 - update) * held + update * candidate).astype(jnp.bfloat16))


def late_kernel(lag, *refs):
    own, first, second, pre_r, pre_u = refs[0:5]
    x0, x1 = refs[5:8], refs[8:11]
    wg, wc, bias, out, wide, wide_r = refs[11:17]

    def store(row, value):
        out[row] = value

    def work():
        late_body(
            lag, own, first, second, (pre_r, pre_u), x0, x1, wg, wc, bias, wide, wide_r, store
        )

    where_active(lag, work)
    if lag == 0:
        @pl.when(lax.axis_index("layer") == 1)
        def _():
            out[...] = own[...]


def last_kernel(*refs):
    own, first, second, pre_r, pre_u = refs[0:5]
    x1 = refs[5:8]
    wg, wc, bias, state0, state1, out, wide, wide_r, result, sent = refs[8:18]
    layer = lax.axis_index("layer")

    @pl.when(layer == 0)
    def _():
        copies = [
            pltpu.make_async_copy(state, out.at[frame], sent.at[frame])
            for frame, state in enumerate((state0, state1, own))
        ]
        for copy in copies:
            copy.start()
        for copy in copies:
            copy.wait()

    @pl.when(layer == 1)
    def _():
        copies = [
            pltpu.make_async_copy(state, out.at[frame], sent.at[frame])
            for frame, state in enumerate((state1, own))
        ]
        for copy in copies:
            copy.start()

        def store(row, value):
            result[row] = value
            copy = pltpu.make_async_copy(result.at[row], out.at[2, row], sent.at[2 + row])
            copy.start()
            copies.append(copy)

        late_body(
            3, own, first, second, (pre_r, pre_u), None, x1, wg, wc, bias, wide, wide_r, store
        )
        for copy in copies:
            copy.wait()


HELD = pl.BlockSpec(memory_space=pltpu.VMEM)
ANYWHERE = pl.BlockSpec(memory_space=pl.ANY)


def cost(units, cols, channels):
    return pl.CostEstimate(
        flops=2 * units * cols * channels * 9 * channels, bytes_accessed=1 << 20, transcendentals=0
    )


def wide_rows(rows, cols, channels):
    return pltpu.VMEM((rows, cols, 3 * channels), jnp.bfloat16)


def outside(array):
    return pltpu.with_memory_space_constraint(array, pltpu.HBM)


def pick(initial, rows):
    return pl.pallas_call(
        pick_kernel,
        out_shape=[jax.ShapeDtypeStruct(initial.shape, initial.dtype)] * 2,
        in_specs=[ANYWHERE] * 2,
        out_specs=[HELD] * 2,
        scratch_shapes=[pltpu.SemaphoreType.DMA((2,))],
        compiler_params=pltpu.CompilerParams(vmem_limit_bytes=SMALL_BYTES),
    )(outside(initial), outside(rows))


def stage(wg):
    _, _, depth, width = wg.shape
    return pl.pallas_call(
        stage_kernel,
        out_shape=jax.ShapeDtypeStruct((3, 3, depth // 2, width), wg.dtype),
        in_specs=[ANYWHERE],
        out_specs=HELD,
        scratch_shapes=[pltpu.SemaphoreType.DMA],
        compiler_params=pltpu.CompilerParams(vmem_limit_bytes=SMALL_BYTES),
    )(outside(wg))


def early(lag, state, wg):
    _, cols, channels = state[0].shape
    pre = lambda n: jax.ShapeDtypeStruct((n * cols, channels), jnp.float32)
    return pl.pallas_call(
        functools.partial(early_kernel, lag),
        out_shape=[pre(4), pre(2)],
        in_specs=[HELD] * 4,
        out_specs=[HELD] * 2,
        scratch_shapes=[wide_rows(6, cols, channels)],
        compiler_params=pltpu.CompilerParams(vmem_limit_bytes=VMEM_BYTES),
        cost_estimate=cost(6, cols, channels),
    )(*state, wg)


def late(lag, state, pre, x0, x1, wg, wc, bias):
    _, cols, channels = state[0].shape
    return pl.pallas_call(
        functools.partial(late_kernel, lag),
        out_shape=jax.ShapeDtypeStruct((2, cols, channels), jnp.bfloat16),
        in_specs=[HELD] * 14,
        out_specs=HELD,
        scratch_shapes=[wide_rows(6, cols, channels), wide_rows(4, cols, channels)],
        compiler_params=pltpu.CompilerParams(vmem_limit_bytes=VMEM_BYTES),
        cost_estimate=cost(10, cols, channels),
    )(*state, *pre, *x0, *x1, wg, wc, bias)


def last(state, pre, x1, wg, wc, bias, earlier):
    _, cols, channels = state[0].shape
    return pl.pallas_call(
        last_kernel,
        out_shape=jax.ShapeDtypeStruct((3, 2, cols, channels), jnp.bfloat16),
        in_specs=[HELD] * 13,
        out_specs=ANYWHERE,
        scratch_shapes=[
            wide_rows(6, cols, channels),
            wide_rows(4, cols, channels),
            pltpu.VMEM((2, cols, channels), jnp.bfloat16),
            pltpu.SemaphoreType.DMA((4,)),
        ],
        compiler_params=pltpu.CompilerParams(vmem_limit_bytes=VMEM_BYTES),
        cost_estimate=cost(10, cols, channels),
    )(*state, *pre, *x1, wg, wc, bias, *earlier)


def pair_swap(field, start):
    count = lax.axis_size("rows")
    route = []
    for low in range(start, count - 1, 2):
        route += [(low, low + 1), (low + 1, low)]
    return lax.ppermute(field, "rows", route)


def gathered_swap(field, odd, inner, beside):
    count = lax.axis_size("rows")
    groups = [[0, count], [count - 1, 2 * count - 1]]
    for layer in range(2):
        groups += [[layer * count + low, layer * count + low + 1] for low in range(1, count - 1, 2)]
    both = lax.all_gather(field, ("layer", "rows"), axis_index_groups=groups)
    if beside:
        both, *beside = lax.optimization_barrier((both, *beside))
    partner = jnp.where(odd, both[1], both[0])
    return jnp.where(inner, partner, jnp.zeros_like(partner)), *beside


def across(field):
    return lax.ppermute(field, "layer", [(0, 1), (1, 0)])


def shards(frames, initial_state, w_gates, w_cand, biases):
    strip = lax.axis_index("rows")
    wg, wc = w_gates[0], w_cand[0]
    hidden = initial_state[0]
    rows = frames.reshape((6,) + hidden.shape[1:])

    odd = lax.rem(strip, 2) == 1
    inner = jnp.logical_and(strip > 0, strip < lax.axis_size("rows") - 1)
    field, later_field = pick(hidden, rows)
    field, odd, inner = lax.optimization_barrier((field, odd, inner))
    second = pair_swap(field, 1)
    first = pair_swap(field, 0)
    wg_state = stage(wg)
    late_second = pair_swap(later_field, 1)
    late_first = pair_swap(later_field, 0)
    second_after, wg_state = lax.optimization_barrier((second, wg_state))
    halos = [
        (across(first), across(second_after)),
        (late_first, late_second),
        (across(late_first), across(late_second)),
    ]
    below = (field, first, second)
    pre = early(0, below, wg_state)
    pre = lax.optimization_barrier((*pre, late_second, late_first))[0:2]
    hidden = late(0, (hidden, first, second), pre, (rows, *halos[0]), below, wg, wc, biases)
    states = [hidden]
    for step in range(1, 4):
        first = pair_swap(hidden, 0)
        own_below = across(hidden)
        beside = (first, own_below) if step > 1 else ()
        second, *beside = gathered_swap(hidden, odd, inner, beside)
        first, own_below = beside or (first, own_below)
        below = (own_below, across(first), across(second))
        state = (hidden, first, second)
        pre = early(step, state, wg_state)
        if step == 3:
            return last(state, pre, below, wg, wc, biases, states[0:2])[None]
        hidden = late(step, state, pre, (rows, *halos[step]), below, wg, wc, biases)
        states.append(hidden)


def solution(mesh):
    placed = (
        P(None, "rows", None, None),
        P("layer", "rows", None, None),
        P("layer", None, None, None, None),
        P("layer", None, None, None, None),
        P("layer", None),
    )
    return jax.shard_map(
        shards,
        mesh=mesh,
        in_specs=placed,
        out_specs=P("layer", None, "rows", None, None),
        check_vma=False,
    )
```

```python
import functools

import jax
import jax.numpy as jnp
from jax import lax
from jax.experimental import pallas as pl
from jax.experimental.pallas import tpu as pltpu
from jax.sharding import PartitionSpec as P

VMEM_BYTES = 16 * 1024 * 1024
SMALL_BYTES = 8 * 1024 * 1024


def widen(target, row, value):
    cols, channels = value.shape
    wide = value.astype(jnp.float32)
    position = lax.broadcasted_iota(jnp.int32, (cols, channels), 0)
    left = jnp.where(position == 0, 0.0, pltpu.roll(wide, 1, 0))
    right = jnp.where(position == cols - 1, 0.0, pltpu.roll(wide, cols - 1, 0))
    target[row, :, 0:channels] = left.astype(jnp.bfloat16)
    target[row, :, channels : 2 * channels] = value
    target[row, :, 2 * channels : 3 * channels] = right.astype(jnp.bfloat16)


def halo_row(first, second, odd, row):
    one, other = first[row % 2], second[row % 2]
    return jnp.where(odd == (row < 2), one, other)


def spread(own, first, second, base=0):
    odd = is_odd()
    return (
        [functools.partial(halo_row, first, second, odd, row) for row in range(2)]
        + [functools.partial(lambda row: own[base + row], row) for row in range(2)]
        + [functools.partial(halo_row, first, second, odd, row) for row in range(2, 4)]
    )


def fill(target, rows):
    for row, value in enumerate(rows):
        widen(target, row, value())


def taps(source, start, rows):
    _, cols, width = source.shape
    return jnp.concatenate(
        [source[start + tap : start + tap + rows].reshape(rows * cols, width) for tap in range(3)],
        -1,
    )


def columns(weight, lo, channels, out_lo, out_hi):
    return weight[:, :, lo : lo + channels, out_lo:out_hi].reshape(9 * channels, out_hi - out_lo)


def product(left, right):
    return jnp.dot(left, right, preferred_element_type=jnp.float32)


def where_active(lag, work):
    if lag in (0, 3):
        pl.when(lax.axis_index("layer") == (0 if lag == 0 else 1))(work)
    else:
        work()


def is_odd():
    return lax.rem(lax.axis_index("rows"), 2) == 1


def state_load(weight, state_weight, ready):
    channels = weight.shape[2] // 2
    return pltpu.make_async_copy(weight.at[:, :, channels : 2 * channels], state_weight, ready)


def pick_kernel(initial, frames, weight, out, later, state_weight, ready):
    for wanted, sources in enumerate(
        ((initial, frames.at[2:4]), (frames.at[0:2], frames.at[4:6]))
    ):
        @pl.when(lax.axis_index("layer") == wanted)
        def _():
            if wanted == 1:
                load = state_load(weight, state_weight, ready.at[2])
                load.start()
                load.wait()
            copies = [
                pltpu.make_async_copy(source, target, ready.at[i])
                for i, (source, target) in enumerate(zip(sources, (out, later)))
            ]
            for copy in copies:
                copy.start()
            for copy in copies:
                copy.wait()


def stage_kernel(weight, given, state_weight, ready):
    @pl.when(lax.axis_index("layer") == 0)
    def _():
        load = state_load(weight, state_weight, ready)
        load.start()
        load.wait()


def early_kernel(lag, own, first, second, wg, pre_r, pre_u, wide):
    cols, channels = own.shape[1:]

    def work():
        fill(wide, spread(own, first, second))
        inner = product(taps(wide, 1, 2), columns(wg, 0, channels, 0, 2 * channels))
        edges = jnp.concatenate([taps(wide, 0, 1), taps(wide, 3, 1)], 0)
        outer = product(edges, columns(wg, 0, channels, channels, 2 * channels))
        pre_u[...] = inner[:, 0:channels]
        pre_r[cols : 3 * cols] = inner[:, channels : 2 * channels]
        pre_r[0:cols] = outer[0:cols]
        pre_r[3 * cols : 4 * cols] = outer[cols : 2 * cols]

    where_active(lag, work)


def late_body(lag, own, first, second, pre, x0, x1, wg, wc, bias, wide, wide_r, store):
    cols, channels = own.shape[1:]
    odd = is_odd()
    if lag == 0:
        fill(wide, spread(*x0))
    elif lag == 3:
        fill(wide, spread(*x1))
    else:
        lower = lax.axis_index("layer") == 0
        for row, (one, other) in enumerate(zip(spread(*x0, 2 * lag), spread(*x1))):
            widen(wide, row, jnp.where(lower, one(), other()))

    of_reset = product(taps(wide, 0, 4), columns(wg, 0, channels, channels, 2 * channels))
    for row in range(4):
        part = slice(row * cols, (row + 1) * cols)
        held = own[row - 1] if 0 < row < 3 else halo_row(first, second, odd, 1 if row == 0 else 2)
        gate = jax.nn.sigmoid(
            pre[0][part] + of_reset[part] + bias[:, channels : 2 * channels]
        )
        widen(wide_r, row, (gate * held.astype(jnp.float32)).astype(jnp.bfloat16))
    weight = jnp.concatenate(
        [columns(wg, 0, channels, 0, channels), columns(wc, 0, channels, 0, channels)], -1
    )
    inner = product(taps(wide, 1, 2), weight)
    sum_u = pre[1][...] + inner[:, 0:channels]
    sum_c = inner[:, channels : 2 * channels] + product(
        taps(wide_r, 0, 2), columns(wc, channels, channels, 0, channels)
    )
    for row in range(2):
        part = slice(row * cols, (row + 1) * cols)
        held = own[row].astype(jnp.float32)
        update = jax.nn.sigmoid(sum_u[part] + bias[:, 0:channels])
        candidate = jnp.tanh(sum_c[part] + bias[:, 2 * channels : 3 * channels])
        store(row, ((1.0 - update) * held + update * candidate).astype(jnp.bfloat16))


def late_kernel(lag, *refs):
    own, first, second, pre_r, pre_u = refs[0:5]
    x0, x1 = refs[5:8], refs[8:11]
    wg, wc, bias, out, wide, wide_r = refs[11:17]

    def store(row, value):
        out[row] = value

    def work():
        late_body(
            lag, own, first, second, (pre_r, pre_u), x0, x1, wg, wc, bias, wide, wide_r, store
        )

    where_active(lag, work)
    if lag == 0:
        @pl.when(lax.axis_index("layer") == 1)
        def _():
            out[...] = own[...]


def last_kernel(*refs):
    own, first, second, pre_r, pre_u = refs[0:5]
    x1 = refs[5:8]
    wg, wc, bias, state0, state1, out, wide, wide_r, result, sent = refs[8:18]
    layer = lax.axis_index("layer")

    @pl.when(layer == 0)
    def _():
        copies = [
            pltpu.make_async_copy(state, out.at[frame], sent.at[frame])
            for frame, state in enumerate((state0, state1, own))
        ]
        for copy in copies:
            copy.start()
        for copy in copies:
            copy.wait()

    @pl.when(layer == 1)
    def _():
        copies = [
            pltpu.make_async_copy(state, out.at[frame], sent.at[frame])
            for frame, state in enumerate((state1, own))
        ]
        for copy in copies:
            copy.start()

        def store(row, value):
            result[row] = value
            copy = pltpu.make_async_copy(result.at[row], out.at[2, row], sent.at[2 + row])
            copy.start()
            copies.append(copy)

        late_body(
            3, own, first, second, (pre_r, pre_u), None, x1, wg, wc, bias, wide, wide_r, store
        )
        for copy in copies:
            copy.wait()


HELD = pl.BlockSpec(memory_space=pltpu.VMEM)
ANYWHERE = pl.BlockSpec(memory_space=pl.ANY)


def cost(units, cols, channels):
    return pl.CostEstimate(
        flops=2 * units * cols * channels * 9 * channels, bytes_accessed=1 << 20, transcendentals=0
    )


def wide_rows(rows, cols, channels):
    return pltpu.VMEM((rows, cols, 3 * channels), jnp.bfloat16)


def outside(array):
    return pltpu.with_memory_space_constraint(array, pltpu.HBM)


def pick(initial, rows, wg):
    _, _, depth, width = wg.shape
    return pl.pallas_call(
        pick_kernel,
        out_shape=[jax.ShapeDtypeStruct(initial.shape, initial.dtype)] * 2
        + [jax.ShapeDtypeStruct((3, 3, depth // 2, width), wg.dtype)],
        in_specs=[ANYWHERE] * 3,
        out_specs=[HELD] * 3,
        scratch_shapes=[pltpu.SemaphoreType.DMA((3,))],
        compiler_params=pltpu.CompilerParams(vmem_limit_bytes=SMALL_BYTES),
    )(outside(initial), outside(rows), outside(wg))


def stage(wg, given):
    return pl.pallas_call(
        stage_kernel,
        out_shape=jax.ShapeDtypeStruct(given.shape, given.dtype),
        in_specs=[ANYWHERE, HELD],
        out_specs=HELD,
        scratch_shapes=[pltpu.SemaphoreType.DMA],
        input_output_aliases={1: 0},
        compiler_params=pltpu.CompilerParams(vmem_limit_bytes=SMALL_BYTES),
    )(outside(wg), given)


def early(lag, state, wg):
    _, cols, channels = state[0].shape
    pre = lambda n: jax.ShapeDtypeStruct((n * cols, channels), jnp.float32)
    return pl.pallas_call(
        functools.partial(early_kernel, lag),
        out_shape=[pre(4), pre(2)],
        in_specs=[HELD] * 4,
        out_specs=[HELD] * 2,
        scratch_shapes=[wide_rows(6, cols, channels)],
        compiler_params=pltpu.CompilerParams(vmem_limit_bytes=VMEM_BYTES),
        cost_estimate=cost(6, cols, channels),
    )(*state, wg)


def late(lag, state, pre, x0, x1, wg, wc, bias):
    _, cols, channels = state[0].shape
    return pl.pallas_call(
        functools.partial(late_kernel, lag),
        out_shape=jax.ShapeDtypeStruct((2, cols, channels), jnp.bfloat16),
        in_specs=[HELD] * 14,
        out_specs=HELD,
        scratch_shapes=[wide_rows(6, cols, channels), wide_rows(4, cols, channels)],
        compiler_params=pltpu.CompilerParams(vmem_limit_bytes=VMEM_BYTES),
        cost_estimate=cost(10, cols, channels),
    )(*state, *pre, *x0, *x1, wg, wc, bias)


def last(state, pre, x1, wg, wc, bias, earlier):
    _, cols, channels = state[0].shape
    return pl.pallas_call(
        last_kernel,
        out_shape=jax.ShapeDtypeStruct((3, 2, cols, channels), jnp.bfloat16),
        in_specs=[HELD] * 13,
        out_specs=ANYWHERE,
        scratch_shapes=[
            wide_rows(6, cols, channels),
            wide_rows(4, cols, channels),
            pltpu.VMEM((2, cols, channels), jnp.bfloat16),
            pltpu.SemaphoreType.DMA((4,)),
        ],
        compiler_params=pltpu.CompilerParams(vmem_limit_bytes=VMEM_BYTES),
        cost_estimate=cost(10, cols, channels),
    )(*state, *pre, *x1, wg, wc, bias, *earlier)


def pair_swap(field, start):
    count = lax.axis_size("rows")
    route = []
    for low in range(start, count - 1, 2):
        route += [(low, low + 1), (low + 1, low)]
    return lax.ppermute(field, "rows", route)


def gathered_swap(field, odd, inner, beside):
    count = lax.axis_size("rows")
    groups = [[0, count], [count - 1, 2 * count - 1]]
    for layer in range(2):
        groups += [[layer * count + low, layer * count + low + 1] for low in range(1, count - 1, 2)]
    both = lax.all_gather(field, ("layer", "rows"), axis_index_groups=groups)
    if beside is not None:
        both, beside = lax.optimization_barrier((both, beside))
    partner = jnp.where(odd, both[1], both[0])
    return jnp.where(inner, partner, jnp.zeros_like(partner)), beside


def across(field):
    return lax.ppermute(field, "layer", [(0, 1), (1, 0)])


def shards(frames, initial_state, w_gates, w_cand, biases):
    strip = lax.axis_index("rows")
    wg, wc = w_gates[0], w_cand[0]
    hidden = initial_state[0]
    rows = frames.reshape((6,) + hidden.shape[1:])

    odd = lax.rem(strip, 2) == 1
    inner = jnp.logical_and(strip > 0, strip < lax.axis_size("rows") - 1)
    field, later_field, wg_state = pick(hidden, rows, wg)
    field, odd, inner = lax.optimization_barrier((field, odd, inner))
    second = pair_swap(field, 1)
    first = pair_swap(field, 0)
    wg_state = stage(wg, wg_state)
    late_second = pair_swap(later_field, 1)
    late_first = pair_swap(later_field, 0)
    second_after, wg_state = lax.optimization_barrier((second, wg_state))
    halos = [
        (across(first), across(second_after)),
        (late_first, late_second),
        (across(late_first), across(late_second)),
    ]
    below = (field, first, second)
    pre = early(0, below, wg_state)
    pre = lax.optimization_barrier((*pre, late_second, late_first))[0:2]
    hidden = late(0, (hidden, first, second), pre, (rows, *halos[0]), below, wg, wc, biases)
    states = [hidden]
    for step in range(1, 4):
        first = pair_swap(hidden, 0)
        own_below = across(hidden)
        second, waited = gathered_swap(hidden, odd, inner, own_below if step > 1 else None)
        own_below = waited if step > 1 else own_below
        below = (own_below, across(first), across(second))
        state = (hidden, first, second)
        pre = early(step, state, wg_state)
        if step == 3:
            return last(state, pre, below, wg, wc, biases, states[0:2])[None]
        hidden = late(step, state, pre, (rows, *halos[step]), below, wg, wc, biases)
        states.append(hidden)


def solution(mesh):
    placed = (
        P(None, "rows", None, None),
        P("layer", "rows", None, None),
        P("layer", None, None, None, None),
        P("layer", None, None, None, None),
        P("layer", None),
    )
    return jax.shard_map(
        shards,
        mesh=mesh,
        in_specs=placed,
        out_specs=P("layer", None, "rows", None, None),
        check_vma=False,
    )
```

```python
import functools

import jax
import jax.numpy as jnp
from jax import lax
from jax.experimental import pallas as pl
from jax.experimental.pallas import tpu as pltpu
from jax.sharding import PartitionSpec as P

VMEM_BYTES = 16 * 1024 * 1024
SMALL_BYTES = 8 * 1024 * 1024


def widen(target, row, value):
    cols, channels = value.shape
    wide = value.astype(jnp.float32)
    position = lax.broadcasted_iota(jnp.int32, (cols, channels), 0)
    left = jnp.where(position == 0, 0.0, pltpu.roll(wide, 1, 0))
    right = jnp.where(position == cols - 1, 0.0, pltpu.roll(wide, cols - 1, 0))
    target[row, :, 0:channels] = left.astype(jnp.bfloat16)
    target[row, :, channels : 2 * channels] = value
    target[row, :, 2 * channels : 3 * channels] = right.astype(jnp.bfloat16)


def halo_row(first, second, odd, row):
    one, other = first[row % 2], second[row % 2]
    return jnp.where(odd == (row < 2), one, other)


def spread(own, first, second, base=0):
    odd = is_odd()
    return (
        [functools.partial(halo_row, first, second, odd, row) for row in range(2)]
        + [functools.partial(lambda row: own[base + row], row) for row in range(2)]
        + [functools.partial(halo_row, first, second, odd, row) for row in range(2, 4)]
    )


def fill(target, rows):
    for row, value in enumerate(rows):
        widen(target, row, value())


def taps(source, start, rows):
    _, cols, width = source.shape
    return jnp.concatenate(
        [source[start + tap : start + tap + rows].reshape(rows * cols, width) for tap in range(3)],
        -1,
    )


def columns(weight, lo, channels, out_lo, out_hi):
    return weight[:, :, lo : lo + channels, out_lo:out_hi].reshape(9 * channels, out_hi - out_lo)


def product(left, right):
    return jnp.dot(left, right, preferred_element_type=jnp.float32)


def where_active(lag, work):
    if lag in (0, 3):
        pl.when(lax.axis_index("layer") == (0 if lag == 0 else 1))(work)
    else:
        work()


def is_odd():
    return lax.rem(lax.axis_index("rows"), 2) == 1


def pick_kernel(initial, frames, out, later, ready):
    for wanted, sources in enumerate(
        ((initial, frames.at[2:4]), (frames.at[0:2], frames.at[4:6]))
    ):
        @pl.when(lax.axis_index("layer") == wanted)
        def _():
            copies = [
                pltpu.make_async_copy(source, target, ready.at[i])
                for i, (source, target) in enumerate(zip(sources, (out, later)))
            ]
            for copy in copies:
                copy.start()
            for copy in copies:
                copy.wait()


def stage_kernel(weight, state_weight, ready):
    channels = weight.shape[2] // 2
    load = pltpu.make_async_copy(weight.at[:, :, channels : 2 * channels], state_weight, ready)
    load.start()
    load.wait()


def early_kernel(lag, own, first, second, wg, pre_r, pre_u, wide):
    cols, channels = own.shape[1:]

    def work():
        fill(wide, spread(own, first, second))
        inner = product(taps(wide, 1, 2), columns(wg, 0, channels, 0, 2 * channels))
        edges = jnp.concatenate([taps(wide, 0, 1), taps(wide, 3, 1)], 0)
        outer = product(edges, columns(wg, 0, channels, channels, 2 * channels))
        pre_u[...] = inner[:, 0:channels]
        pre_r[cols : 3 * cols] = inner[:, channels : 2 * channels]
        pre_r[0:cols] = outer[0:cols]
        pre_r[3 * cols : 4 * cols] = outer[cols : 2 * cols]

    where_active(lag, work)


def late_body(lag, own, first, second, pre, x0, x1, wg, wc, bias, wide, wide_r, store):
    cols, channels = own.shape[1:]
    odd = is_odd()
    if lag == 0:
        fill(wide, spread(*x0))
    elif lag == 3:
        fill(wide, spread(*x1))
    else:
        lower = lax.axis_index("layer") == 0
        for row, (one, other) in enumerate(zip(spread(*x0, 2 * lag), spread(*x1))):
            widen(wide, row, jnp.where(lower, one(), other()))

    of_reset = product(taps(wide, 0, 4), columns(wg, 0, channels, channels, 2 * channels))
    for row in range(4):
        part = slice(row * cols, (row + 1) * cols)
        held = own[row - 1] if 0 < row < 3 else halo_row(first, second, odd, 1 if row == 0 else 2)
        gate = jax.nn.sigmoid(
            pre[0][part] + of_reset[part] + bias[:, channels : 2 * channels]
        )
        widen(wide_r, row, (gate * held.astype(jnp.float32)).astype(jnp.bfloat16))
    weight = jnp.concatenate(
        [columns(wg, 0, channels, 0, channels), columns(wc, 0, channels, 0, channels)], -1
    )
    inner = product(taps(wide, 1, 2), weight)
    sum_u = pre[1][...] + inner[:, 0:channels]
    sum_c = inner[:, channels : 2 * channels] + product(
        taps(wide_r, 0, 2), columns(wc, channels, channels, 0, channels)
    )
    for row in range(2):
        part = slice(row * cols, (row + 1) * cols)
        held = own[row].astype(jnp.float32)
        update = jax.nn.sigmoid(sum_u[part] + bias[:, 0:channels])
        candidate = jnp.tanh(sum_c[part] + bias[:, 2 * channels : 3 * channels])
        store(row, ((1.0 - update) * held + update * candidate).astype(jnp.bfloat16))


def late_kernel(lag, *refs):
    own, first, second, pre_r, pre_u = refs[0:5]
    x0, x1 = refs[5:8], refs[8:11]
    wg, wc, bias, out, wide, wide_r = refs[11:17]

    def store(row, value):
        out[row] = value

    def work():
        late_body(
            lag, own, first, second, (pre_r, pre_u), x0, x1, wg, wc, bias, wide, wide_r, store
        )

    where_active(lag, work)
    if lag == 0:
        @pl.when(lax.axis_index("layer") == 1)
        def _():
            out[...] = own[...]


def last_kernel(*refs):
    own, first, second, pre_r, pre_u = refs[0:5]
    x1 = refs[5:8]
    wg, wc, bias, state0, state1, out, wide, wide_r, result, sent = refs[8:18]
    layer = lax.axis_index("layer")

    @pl.when(layer == 0)
    def _():
        copies = [
            pltpu.make_async_copy(state, out.at[frame], sent.at[frame])
            for frame, state in enumerate((state0, state1, own))
        ]
        for copy in copies:
            copy.start()
        for copy in copies:
            copy.wait()

    @pl.when(layer == 1)
    def _():
        copies = [
            pltpu.make_async_copy(state, out.at[frame], sent.at[frame])
            for frame, state in enumerate((state1, own))
        ]
        for copy in copies:
            copy.start()

        def store(row, value):
            result[row] = value
            copy = pltpu.make_async_copy(result.at[row], out.at[2, row], sent.at[2 + row])
            copy.start()
            copies.append(copy)

        late_body(
            3, own, first, second, (pre_r, pre_u), None, x1, wg, wc, bias, wide, wide_r, store
        )
        for copy in copies:
            copy.wait()


HELD = pl.BlockSpec(memory_space=pltpu.VMEM)
ANYWHERE = pl.BlockSpec(memory_space=pl.ANY)


def cost(units, cols, channels):
    return pl.CostEstimate(
        flops=2 * units * cols * channels * 9 * channels, bytes_accessed=1 << 20, transcendentals=0
    )


def wide_rows(rows, cols, channels):
    return pltpu.VMEM((rows, cols, 3 * channels), jnp.bfloat16)


def outside(array):
    return pltpu.with_memory_space_constraint(array, pltpu.HBM)


def pick(initial, rows):
    return pl.pallas_call(
        pick_kernel,
        out_shape=[jax.ShapeDtypeStruct(initial.shape, initial.dtype)] * 2,
        in_specs=[ANYWHERE] * 2,
        out_specs=[HELD] * 2,
        scratch_shapes=[pltpu.SemaphoreType.DMA((2,))],
        compiler_params=pltpu.CompilerParams(vmem_limit_bytes=SMALL_BYTES),
    )(outside(initial), outside(rows))


def stage(wg):
    _, _, depth, width = wg.shape
    return pl.pallas_call(
        stage_kernel,
        out_shape=jax.ShapeDtypeStruct((3, 3, depth // 2, width), wg.dtype),
        in_specs=[ANYWHERE],
        out_specs=HELD,
        scratch_shapes=[pltpu.SemaphoreType.DMA],
        compiler_params=pltpu.CompilerParams(vmem_limit_bytes=SMALL_BYTES),
    )(outside(wg))


def early(lag, state, wg):
    _, cols, channels = state[0].shape
    pre = lambda n: jax.ShapeDtypeStruct((n * cols, channels), jnp.float32)
    return pl.pallas_call(
        functools.partial(early_kernel, lag),
        out_shape=[pre(4), pre(2)],
        in_specs=[HELD] * 4,
        out_specs=[HELD] * 2,
        scratch_shapes=[wide_rows(6, cols, channels)],
        compiler_params=pltpu.CompilerParams(vmem_limit_bytes=VMEM_BYTES),
        cost_estimate=cost(6, cols, channels),
    )(*state, wg)


def late(lag, state, pre, x0, x1, wg, wc, bias):
    _, cols, channels = state[0].shape
    return pl.pallas_call(
        functools.partial(late_kernel, lag),
        out_shape=jax.ShapeDtypeStruct((2, cols, channels), jnp.bfloat16),
        in_specs=[HELD] * 14,
        out_specs=HELD,
        scratch_shapes=[wide_rows(6, cols, channels), wide_rows(4, cols, channels)],
        compiler_params=pltpu.CompilerParams(vmem_limit_bytes=VMEM_BYTES),
        cost_estimate=cost(10, cols, channels),
    )(*state, *pre, *x0, *x1, wg, wc, bias)


def last(state, pre, x1, wg, wc, bias, earlier):
    _, cols, channels = state[0].shape
    return pl.pallas_call(
        last_kernel,
        out_shape=jax.ShapeDtypeStruct((3, 2, cols, channels), jnp.bfloat16),
        in_specs=[HELD] * 13,
        out_specs=ANYWHERE,
        scratch_shapes=[
            wide_rows(6, cols, channels),
            wide_rows(4, cols, channels),
            pltpu.VMEM((2, cols, channels), jnp.bfloat16),
            pltpu.SemaphoreType.DMA((4,)),
        ],
        compiler_params=pltpu.CompilerParams(vmem_limit_bytes=VMEM_BYTES),
        cost_estimate=cost(10, cols, channels),
    )(*state, *pre, *x1, wg, wc, bias, *earlier)


def pair_swap(field, start):
    count = lax.axis_size("rows")
    route = []
    for low in range(start, count - 1, 2):
        route += [(low, low + 1), (low + 1, low)]
    return lax.ppermute(field, "rows", route)


def gathered_swap(field, odd, inner, beside):
    count = lax.axis_size("rows")
    groups = [[0, count], [count - 1, 2 * count - 1]]
    for layer in range(2):
        groups += [[layer * count + low, layer * count + low + 1] for low in range(1, count - 1, 2)]
    both = lax.all_gather(field, ("layer", "rows"), axis_index_groups=groups)
    if beside is not None:
        both, beside = lax.optimization_barrier((both, beside))
    partner = jnp.where(odd, both[1], both[0])
    return jnp.where(inner, partner, jnp.zeros_like(partner)), beside


def across(field):
    return lax.ppermute(field, "layer", [(0, 1), (1, 0)])


def shards(frames, initial_state, w_gates, w_cand, biases):
    strip = lax.axis_index("rows")
    wg, wc = w_gates[0], w_cand[0]
    hidden = initial_state[0]
    rows = frames.reshape((6,) + hidden.shape[1:])

    odd = lax.rem(strip, 2) == 1
    inner = jnp.logical_and(strip > 0, strip < lax.axis_size("rows") - 1)
    field, later_field = pick(hidden, rows)
    field, odd, inner = lax.optimization_barrier((field, odd, inner))
    second = pair_swap(field, 1)
    first = pair_swap(field, 0)
    wg_state = stage(wg)
    late_second = pair_swap(later_field, 1)
    late_first = pair_swap(later_field, 0)
    second_after, wg_state = lax.optimization_barrier((second, wg_state))
    halos = [
        (across(first), across(second_after)),
        (late_first, late_second),
    ]
    below = (field, first, second)
    pre = early(0, below, wg_state)
    pre = lax.optimization_barrier((*pre, late_second, late_first))[0:2]
    hidden = late(0, (hidden, first, second), pre, (rows, *halos[0]), below, wg, wc, biases)
    states = [hidden]
    for step in range(1, 4):
        first = pair_swap(hidden, 0)
        own_below = across(hidden)
        second, waited = gathered_swap(hidden, odd, inner, own_below if step > 1 else None)
        own_below = waited if step > 1 else own_below
        below = (own_below, across(first), across(second))
        state = (hidden, first, second)
        pre = early(step, state, wg_state)
        if step == 1:
            passed = lax.optimization_barrier((late_first, late_second, second))[0:2]
            *pre, one, other = lax.optimization_barrier((*pre, *map(across, passed)))
            halos.append((one, other))
        if step == 3:
            return last(state, pre, below, wg, wc, biases, states[0:2])[None]
        hidden = late(step, state, pre, (rows, *halos[step]), below, wg, wc, biases)
        states.append(hidden)


def solution(mesh):
    placed = (
        P(None, "rows", None, None),
        P("layer", "rows", None, None),
        P("layer", None, None, None, None),
        P("layer", None, None, None, None),
        P("layer", None),
    )
    return jax.shard_map(
        shards,
        mesh=mesh,
        in_specs=placed,
        out_specs=P("layer", None, "rows", None, None),
        check_vma=False,
    )
```
